1024 devices in a mesh: node: 128 (over y, z), sub: 8 (over x, core).
Axes of the slice: x: 4, y: 8, z: 16, core: 2. Of those that a mesh axis runs over, the one named last changes fastest.
Arguments:
- right_side: bfloat16 [128, 256, 32, 128], P('node', 'sub'), may hold values from -6 to 6
- diag_blocks: bfloat16 [128, 256, 128, 128], P('node', 'sub'), as said below
- link_blocks: bfloat16 [128, 256, 128, 128], P('node', 'sub'), may hold values from -0.119628906 to 0.119628906
- restrict_map: bfloat16 [128, 128], replicated, may hold values from -0.8984375 to 0.8984375
- level_map: float32 [2, 128, 128], replicated, as said below
- coarse_inverse: float32 [256, 256], replicated, as said below
Outputs:
- relaxed: float32 [128, 256, 32, 128], P('node', 'sub')
- coarse_solution: float32 [128, 8, 32, 256], P('node', 'sub')
The draws below stay inside these ranges and needn't reach their ends.
Inputs may be any that keep to these rules, and one draw needn't show every extreme that they name: diag_blocks are each 2 times the identity plus entries of deviation 0.34 / sqrt(128). level_map blocks are the identity plus entries of deviation 0.2 / sqrt(128). coarse_inverse is the identity plus entries of deviation 0.2 / sqrt(256).
All inputs are finite; a program needn't handle non-finite values.
Results may differ from the reference program's by a relative error of at most 0.0092.
Values may be sent and summed in bfloat16 or wider, within the bound.
No kernel may reach another device: no remote copies, remote signals or barrier semaphores. Data moves between devices by JAX's collectives and lax.ppermute only.
A program may use at most 32 MiB of HBM per device.

```python
import math
import jax
import jax.numpy as jnp
import numpy as np
from jax import lax

ROWS = 128
VECS = 32
TILES = 32
CT = 2
CHAIN = 256
N_NODE = 128
N_SUB = 8


def noise_field(key, shape, deviation):
    return jax.random.normal(key, shape, jnp.float32) * deviation


def draw_diag_blocks(key, part):
    key = jax.random.fold_in(key, 11)
    shape = (N_NODE, TILES * N_SUB, ROWS, ROWS)
    noise = noise_field(key, shape, 0.34 / math.sqrt(ROWS))
    eye = jnp.eye(ROWS, dtype=jnp.float32)
    return (noise + 2.0 * eye).astype(jnp.bfloat16)


def draw_level_map(key, part):
    key = jax.random.fold_in(key, 23)
    noise = noise_field(key, (CT, ROWS, ROWS), 0.2 / math.sqrt(ROWS))
    return noise + jnp.eye(ROWS, dtype=jnp.float32)


def draw_coarse_inverse(key, part):
    key = jax.random.fold_in(key, 37)
    width = CT * ROWS
    noise = noise_field(key, (width, width), 0.2 / math.sqrt(width))
    return noise + jnp.eye(width, dtype=jnp.float32)


def block_scale(rng, dims, split, least, top_value):
    gain = 1.0
    for position, blocks in split:
        steps = jax.random.uniform(jax.random.fold_in(jax.random.fold_in(rng, 6), position), (blocks,), jnp.float32, least / len(split), top_value / len(split))
        gain = gain * jnp.repeat(jnp.exp(steps), dims[position] // blocks).reshape((-1,) + (1,) * (len(dims) - 1 - position))
    return gain


def centred(stream_key, shape, scale, limit, cuts=(), kind=jnp.bfloat16):
    entries = scale * jax.random.normal(stream_key, shape, jnp.float32)
    if cuts:
        entries = entries * block_scale(stream_key, shape, cuts, -0.22, 0.18)
    return jnp.clip(entries, -limit, limit).astype(kind)


def setup_inputs(seed: int = 0) -> dict:
    keys = jax.random.split(jax.random.key(seed), 7)
    right_side = centred(keys[0], (N_NODE, CHAIN, VECS, ROWS), 1.0, 6.0, ((0, 128), (1, 8)))
    diag_blocks = draw_diag_blocks(jax.random.fold_in(keys[6], 71), 0)
    link_blocks = centred(keys[2], (N_NODE, CHAIN, ROWS, ROWS), 0.02, 0.119628906, ((0, 128), (1, 8)))
    restrict_map = centred(keys[3], (ROWS, ROWS), 0.15, 0.8984375)
    level_map = draw_level_map(jax.random.fold_in(keys[6], 71), 0)
    coarse_inverse = draw_coarse_inverse(jax.random.fold_in(keys[6], 71), 0)
    return dict(right_side=right_side, diag_blocks=diag_blocks, link_blocks=link_blocks, restrict_map=restrict_map, level_map=level_map, coarse_inverse=coarse_inverse)


def apply_chain(field, diag_part, link_part):
    vals = field.astype(jnp.float32)
    diag_f = diag_part.astype(jnp.float32)
    link_f = link_part.astype(jnp.float32)
    zeros_tile = jnp.zeros_like(vals[:1])
    prev_vals = jnp.concatenate([zeros_tile, vals[:-1]], axis=0)
    next_vals = jnp.concatenate([vals[1:], zeros_tile], axis=0)
    prev_link = jnp.concatenate([jnp.zeros_like(link_f[:1]), link_f[:-1]], axis=0)
    total = jnp.einsum('mvr,mrs->mvs', vals, diag_f)
    total = total + jnp.einsum('mvr,mrs->mvs', prev_vals, prev_link)
    total = total + jnp.einsum('mvs,mrs->mvr', next_vals, link_f)
    return total

def relax_chain(inputs):
    rhs_part, diag_part, link_part = inputs
    theta = 2.0
    delta = 1.7
    sigma = theta / delta
    rho = 1.0 / sigma
    residue = rhs_part.astype(jnp.float32)
    direction = residue / theta
    relaxed = direction
    for step in range(4):
        residue = residue - apply_chain(direction.astype(jnp.bfloat16), diag_part, link_part)
        if step < 3:
            rho_new = 1.0 / (2.0 * sigma - rho)
            direction = rho_new * rho * direction + 2.0 * rho_new / delta * residue
            relaxed = relaxed + direction
            rho = rho_new
    return (relaxed, residue)

def reference(right_side, diag_blocks, link_blocks, restrict_map, level_map, coarse_inverse):
    relaxed, residue = lax.map(relax_chain, (right_side, diag_blocks, link_blocks))
    resb = residue.astype(jnp.bfloat16)
    projected = jnp.dot(resb.reshape(-1, ROWS), restrict_map, preferred_element_type=jnp.float32)
    projected = projected.reshape(N_NODE, N_SUB, CT, TILES // CT, VECS, ROWS)
    coarse = lax.optimization_barrier(jnp.sum(projected, axis=3))
    scale = 1.0 / math.sqrt(2.0)
    for bit in range(N_SUB.bit_length() - 1):
        order = np.arange(N_SUB) ^ 1 << bit
        coarse = (coarse + coarse[:, order]) * scale
        coarse = jnp.einsum('nmcvr,crs->nmcvs', coarse, level_map, precision=lax.Precision.HIGHEST)
    for bit in range(N_NODE.bit_length() - 1):
        order = np.arange(N_NODE) ^ 1 << bit
        coarse = (coarse + coarse[order]) * scale
        coarse = jnp.einsum('nmcvr,crs->nmcvs', coarse, level_map, precision=lax.Precision.HIGHEST)
    flat = jnp.transpose(coarse[0, 0], (1, 0, 2)).reshape(VECS, CT * ROWS)
    solved = jnp.dot(flat, coarse_inverse, precision=lax.Precision.HIGHEST, preferred_element_type=jnp.float32)
    coarse_solution = jnp.broadcast_to(solved[None, None], (N_NODE, N_SUB, VECS, CT * ROWS))
    return (relaxed, coarse_solution)
```

```python
import functools
import math

import jax
import jax.numpy as jnp
from jax import lax
from jax.experimental import pallas as pl
from jax.experimental.pallas import tpu as pltpu
from jax.sharding import Mesh
from jax.sharding import PartitionSpec as P

TILES = 32
VECS = 32
ROWS = 128
STEPS = 4
HALF = TILES // 2


def coefficients():
    theta, delta = 2.0, 1.7
    sigma = theta / delta
    rho = 1.0 / sigma
    out = []
    for _ in range(STEPS - 1):
        rho_new = 1.0 / (2.0 * sigma - rho)
        out.append((rho_new * rho, 2.0 * rho_new / delta))
        rho = rho_new
    return out


COEFS = coefficients()


def times(a, b):
    return jnp.dot(a, b, preferred_element_type=jnp.float32)


def times_t(a, b):
    return lax.dot_general(a, b, (((1,), (1,)), ((), ())), preferred_element_type=jnp.float32)


def inner_kernel(rhs, diag, link, rel, state, near, sums, resid, direc, dirb):
    for t in range(TILES):
        r = rhs[t].astype(jnp.float32)
        resid[t] = r
        d = r * 0.5
        direc[t] = d
        rel[t] = d
        dirb[0, t] = d.astype(jnp.bfloat16)
    totals = [jnp.zeros((VECS, ROWS), jnp.float32) for _ in range(2)]
    for k in range(1, STEPS + 1):
        now, later = (k - 1) % 2, k % 2
        near[k - 1] = dirb[now, k]
        near[STEPS + k - 1] = dirb[now, TILES - 1 - k]
        for t in range(k, TILES - k):
            a = times(dirb[now, t], diag[t])
            a = a + times(dirb[now, t - 1], link[t - 1])
            a = a + times_t(dirb[now, t + 1], link[t])
            r = resid[t] - a
            resid[t] = r
            if k < STEPS:
                c0, c1 = COEFS[k - 1]
                d = c0 * direc[t] + c1 * r
                direc[t] = d
                rel[t] = rel[t] + d
                dirb[later, t] = d.astype(jnp.bfloat16)
            else:
                totals[t // HALF] += r.astype(jnp.bfloat16).astype(jnp.float32)
    for i, t in enumerate((0, 1, 2, 3, 31, 30, 29, 28)):
        state[0, i] = resid[t]
        state[1, i] = direc[t]
        state[2, i] = rel[t]
    for c in range(2):
        sums[c] = totals[c]


def edge_kernel(flag, lo, hi, diag_lo, link_lo, diag_hi, link_hi, state, near, sums_in, edge, sums):
    def blocks(ref, base, count, height):
        return [ref[base + i * height : base + (i + 1) * height, :] for i in range(count)]

    def sweep_side(rhs, diag, fwd, near_base, state_base, mirrored):
        res, dirs, rel = {}, {}, {}
        for p in range(4):
            r = rhs[p].astype(jnp.float32)
            res[p] = r
            dirs[p] = r * 0.5
        for i in range(4):
            res[4 + i] = state[0, state_base + i]
            dirs[4 + i] = state[1, state_base + i]
            rel[4 + i] = state[2, state_base + i]
        outward = times if mirrored else times_t
        inward = times_t if mirrored else times
        for k in range(1, STEPS + 1):
            bf = {p: dirs[p].astype(jnp.bfloat16) for p in range(k - 1, k + 4)}
            bf[k + 4] = near[near_base + k - 1]
            for p in range(k, k + 4):
                a = times(bf[p], diag[p])
                a = a + inward(bf[p - 1], fwd[p - 1])
                a = a + outward(bf[p + 1], fwd[p])
                r = res[p] - a
                res[p] = r
                if k < STEPS:
                    c0, c1 = COEFS[k - 1]
                    dirs[p] = c0 * dirs[p] + c1 * r
                    if p >= 4:
                        rel[p] = rel[p] + dirs[p]
        total = jnp.zeros((VECS, ROWS), jnp.float32)
        for i in range(4):
            total = total + res[4 + i].astype(jnp.bfloat16).astype(jnp.float32)
            edge[state_base + i] = rel[4 + i]
        return total

    n = 4 * VECS
    rhs_l = blocks(lo, 0, 4, VECS)
    diag_l = [None] + blocks(lo, n, 3, ROWS) + [diag_lo[i] for i in range(4)]
    fwd_l = blocks(lo, n + 3 * ROWS, 4, ROWS) + [link_lo[i] for i in range(4)]
    total_l = sweep_side(rhs_l, diag_l, fwd_l, 0, 0, False)
    sums[0] = sums_in[0] + total_l
    rhs_r = blocks(hi, 0, 4, VECS)[::-1]
    diag_r = [None] + blocks(hi, n, 3, ROWS)[::-1] + [diag_hi[3 - i] for i in range(4)]
    last = link_hi[4]
    last = jnp.where(flag[0] > 0, last, jnp.zeros_like(last))
    fwd_r = blocks(hi, n + 3 * ROWS, 3, ROWS)[::-1] + [last] + [link_hi[3 - i] for i in range(4)]
    total_r = sweep_side(rhs_r, diag_r, fwd_r, 4, 4, True)
    sums[1] = sums_in[1] + total_r


def map_kernel(restrict, level, inverse, out):
    def dot(a, b):
        return jnp.dot(a, b, precision=lax.Precision.HIGHEST, preferred_element_type=jnp.float32)

    scale = 2.0**-5
    r = restrict[...].astype(jnp.float32) * scale
    for c in range(2):
        one = level[c]
        two = dot(one, one)
        four = dot(two, two)
        eight = dot(four, four)
        head = dot(r, two)
        tail = dot(eight, inverse[c * ROWS : (c + 1) * ROWS, :])
        out[c] = dot(head, tail)


def solve_kernel(s, m, out):
    acc = jnp.zeros((VECS, 2 * ROWS), jnp.float32)
    for c in range(2):
        acc = acc + jnp.dot(
            s[c], m[c], precision=lax.Precision.HIGHEST, preferred_element_type=jnp.float32
        )
    out[...] = acc


VMEM = pl.BlockSpec(memory_space=pltpu.VMEM)
SMEM = pl.BlockSpec(memory_space=pltpu.SMEM)
f32 = functools.partial(jax.ShapeDtypeStruct, dtype=jnp.float32)
bf16 = functools.partial(jax.ShapeDtypeStruct, dtype=jnp.bfloat16)


def direct_sum(piece, axis):
    count = lax.axis_size(axis)
    copies = jnp.broadcast_to(piece.astype(jnp.bfloat16)[None], (count,) + piece.shape)
    got = lax.all_to_all(copies, axis, 0, 0, tiled=True)
    return jnp.sum(got.astype(jnp.float32), axis=0)


def total_of(sums):
    sub = ("x", "core")
    flat = sums.reshape(8, 8, ROWS).astype(jnp.bfloat16)
    piece = jnp.sum(lax.all_to_all(flat, sub, 0, 0, tiled=True).astype(jnp.float32), axis=0)
    piece = direct_sum(piece, "y")
    piece = direct_sum(piece, "z")
    copies = jnp.broadcast_to(piece[None], (8,) + piece.shape)
    return lax.all_to_all(copies, sub, 0, 0, tiled=True).reshape(2, VECS, ROWS)


def shards(right_side, diag_blocks, link_blocks, restrict_map, level_map, coarse_inverse):
    rhs, diag, link = right_side[0], diag_blocks[0], link_blocks[0]
    sub = ("x", "core")

    def packed(r, d, k):
        return jnp.concatenate([a.reshape(-1, ROWS) for a in (r, d, k)], axis=0)

    up = [(i, i + 1) for i in range(7)]
    down = [(i + 1, i) for i in range(7)]
    lo = lax.ppermute(packed(rhs[28:], diag[29:], link[28:]), sub, up)
    hi = lax.ppermute(packed(rhs[:4], diag[:3], link[:3]), sub, down)

    rel, state, near, sums = pl.pallas_call(
        inner_kernel,
        out_shape=(
            f32((TILES, VECS, ROWS)),
            f32((3, 8, VECS, ROWS)),
            bf16((8, VECS, ROWS)),
            f32((2, VECS, ROWS)),
        ),
        in_specs=[VMEM] * 3,
        out_specs=(VMEM,) * 4,
        scratch_shapes=[
            pltpu.VMEM((TILES, VECS, ROWS), jnp.float32),
            pltpu.VMEM((TILES, VECS, ROWS), jnp.float32),
            pltpu.VMEM((2, TILES, VECS, ROWS), jnp.bfloat16),
        ],
        compiler_params=pltpu.CompilerParams(vmem_limit_bytes=24 << 20),
        cost_estimate=pl.CostEstimate(flops=4 * 10**8, bytes_accessed=3 << 20, transcendentals=0),
    )(rhs, diag, link)

    maps = pl.pallas_call(
        map_kernel,
        out_shape=f32((2, ROWS, 2 * ROWS)),
        in_specs=[VMEM] * 3,
        out_specs=VMEM,
        compiler_params=pltpu.CompilerParams(vmem_limit_bytes=8 << 20),
        cost_estimate=pl.CostEstimate(flops=4 * 10**8, bytes_accessed=1 << 19, transcendentals=0),
    )(restrict_map, level_map, coarse_inverse)

    j = lax.axis_index("x") * 2 + lax.axis_index("core")
    flag = (j < 7).astype(jnp.int32).reshape(1)
    edge, sums = pl.pallas_call(
        edge_kernel,
        out_shape=(f32((8, VECS, ROWS)), f32((2, VECS, ROWS))),
        in_specs=[SMEM] + [VMEM] * 9,
        out_specs=(VMEM, VMEM),
        compiler_params=pltpu.CompilerParams(vmem_limit_bytes=16 << 20),
        cost_estimate=pl.CostEstimate(flops=10**8, bytes_accessed=1 << 20, transcendentals=0),
    )(flag, lo, hi, diag[:4], link[:4], diag[28:], link[27:], state, near, sums)

    rel = lax.dynamic_update_slice(rel, edge[:4], (0, 0, 0))
    rel = lax.dynamic_update_slice(rel, edge[4:][::-1], (28, 0, 0))

    total = total_of(sums)
    solved = pl.pallas_call(
        solve_kernel,
        out_shape=f32((VECS, 2 * ROWS)),
        in_specs=[VMEM] * 2,
        out_specs=VMEM,
        compiler_params=pltpu.CompilerParams(vmem_limit_bytes=8 << 20),
        cost_estimate=pl.CostEstimate(flops=10**7, bytes_accessed=1 << 18, transcendentals=0),
    )(total, maps)
    return (rel[None], solved[None, None])


def solution(mesh):
    fine = Mesh(mesh.devices.reshape(8, 16, 4, 2), ("y", "z", "x", "core"))
    node, sub = ("y", "z"), ("x", "core")
    big = P(node, sub, None, None)
    return jax.shard_map(
        shards,
        mesh=fine,
        in_specs=(big, big, big, P(), P(), P()),
        out_specs=(big, big),
        check_vma=False,
    )
```

```python
import functools

import jax
import jax.numpy as jnp
from jax import lax
from jax.experimental import pallas as pl
from jax.experimental.pallas import tpu as pltpu
from jax.sharding import Mesh
from jax.sharding import PartitionSpec as P

TILES = 32
VECS = 32
ROWS = 128
STEPS = 4
HALF = TILES // 2
BF16, F32 = jnp.bfloat16, jnp.float32


def coefficients():
    theta, delta = 2.0, 1.7
    sigma = theta / delta
    rho = 1.0 / sigma
    out = []
    for _ in range(STEPS - 1):
        rho_new = 1.0 / (2.0 * sigma - rho)
        out.append((rho_new * rho, 2.0 * rho_new / delta))
        rho = rho_new
    return out


COEFS = coefficients()
VMEM = pl.BlockSpec(memory_space=pltpu.VMEM)
SMEM = pl.BlockSpec(memory_space=pltpu.SMEM)
HBM = pl.BlockSpec(memory_space=pltpu.HBM)
f32 = functools.partial(jax.ShapeDtypeStruct, dtype=F32)
bf16 = functools.partial(jax.ShapeDtypeStruct, dtype=BF16)


def call(kernel, out_shape, in_specs, out_specs, args, scratch=(), mib=8, cost=(0, 0), **kw):
    return pl.pallas_call(
        kernel,
        out_shape=out_shape,
        in_specs=in_specs,
        out_specs=out_specs,
        scratch_shapes=list(scratch),
        compiler_params=pltpu.CompilerParams(vmem_limit_bytes=int(mib * 2**20)),
        cost_estimate=pl.CostEstimate(flops=cost[0], bytes_accessed=cost[1], transcendentals=0),
        **kw,
    )(*args)


def times(a, b):
    return jnp.dot(a, b, preferred_element_type=F32)


def exact(a, b):
    return jnp.dot(a, b, precision=lax.Precision.HIGHEST, preferred_element_type=F32)


def pack_kernel(info, rhs, diag, link, chip, core, sems):
    def send(up, down):
        parts = (
            (rhs.at[7:8], up.at[0:1]),
            (diag.at[29:32], up.at[1:4]),
            (link.at[28:32], up.at[4:8]),
            (rhs.at[0:1], down.at[0:1]),
            (diag.at[0:3], down.at[1:4]),
            (link.at[0:4], down.at[4:8]),
        )
        copies = [pltpu.make_async_copy(a, b, sems.at[i]) for i, (a, b) in enumerate(parts)]
        for c in copies:
            c.start()
        for c in copies:
            c.wait()

    @pl.when(info[0] == 0)
    def _():
        send(core, chip)

    @pl.when(info[0] != 0)
    def _():
        send(chip, core)


def inner_kernel(rhs, diag, link, rel, state, near, sums, resid, direc, dirb, stack):
    for t in range(1, TILES - 1):
        stack[t, 0:ROWS] = link[t - 1]
        stack[t, ROWS : 2 * ROWS] = diag[t]
        stack[t, 2 * ROWS :] = link[t].T
    for t in (0, TILES - 1):
        r = rhs[t].astype(F32)
        resid[t] = r
        direc[t] = r * 0.5
        rel[t] = r * 0.5
    totals = [jnp.zeros((VECS, ROWS), F32) for _ in range(2)]
    for k in range(1, STEPS + 1):
        now, later = (k - 1) % 2, k % 2

        def moved(t):
            return rhs[t] if k == 1 else dirb[now, t]

        near[k - 1] = moved(k) * BF16(0.5) if k == 1 else moved(k)
        near[STEPS + k - 1] = moved(TILES - 1 - k) * BF16(0.5) if k == 1 else moved(TILES - 1 - k)
        for t in range(k, TILES - k):
            v = jnp.concatenate([moved(t - 1), moved(t), moved(t + 1)], axis=1)
            a = times(v, stack[t])
            if k == 1:
                before = rhs[t].astype(F32)
                r = before - 0.5 * a
                d = before * 0.5
                total = d
            else:
                r = resid[t] - a
                d = direc[t] if k < STEPS else None
                total = rel[t] if k < STEPS else None
            if k < STEPS:
                c0, c1 = COEFS[k - 1]
                d = c0 * d + c1 * r
                rel[t] = total + d
                dirb[later, t] = d.astype(BF16)
                resid[t] = r
                if k < STEPS - 1 or t == k or t == TILES - 1 - k:
                    direc[t] = d
            else:
                totals[t // HALF] += r.astype(BF16).astype(F32)
    for i, t in enumerate((0, 1, 2, 3, 31, 30, 29, 28)):
        state[0, i] = resid[t]
        state[1, i] = direc[t]
        state[2, i] = rel[t]
    for c in range(2):
        sums[c] = totals[c]


def edge_kernel(info, chip, core, diag, link, state, near, sums_in, edge, keep, give, stack, rhs):
    mid, end = slice(ROWS, 2 * ROWS), slice(2 * ROWS, 3 * ROWS)

    def fill(lo, hi):
        for i in range(4):
            rhs[0, i] = lo[0, i * VECS : (i + 1) * VECS, :]
            rhs[1, i] = hi[0, (3 - i) * VECS : (4 - i) * VECS, :]
        for p in (1, 2, 3):
            stack[0, p, 0:ROWS] = lo[4 + p - 1]
            stack[0, p, mid] = lo[p]
            stack[0, p, end] = lo[4 + p].T
            stack[1, p, mid] = hi[4 - p]
            stack[1, p, end] = hi[4 + 3 - p].T
        stack[0, 4, 0:ROWS] = lo[7]
        for p in (1, 2):
            stack[1, p, 0:ROWS] = hi[4 + 2 - p]

    @pl.when(info[0] == 0)
    def _():
        fill(chip, core)

    @pl.when(info[0] != 0)
    def _():
        fill(core, chip)

    last = link[TILES - 1]
    stack[1, 3, 0:ROWS] = jnp.where(info[1] > 0, last, jnp.zeros_like(last))
    for p in range(4, 8):
        if p > 4:
            stack[0, p, 0:ROWS] = link[p - 5]
        stack[0, p, mid] = diag[p - 4]
        stack[0, p, end] = link[p - 4].T
        stack[1, p, 0:ROWS] = link[34 - p]
        stack[1, p, mid] = diag[35 - p]
        stack[1, p, end] = link[35 - p].T

    res, dirs, rel = [{}, {}], [{}, {}], [{}, {}]
    for s in range(2):
        for p in range(4):
            r = rhs[s, p].astype(F32)
            res[s][p] = r
            dirs[s][p] = r * 0.5
        for i in range(4):
            res[s][4 + i] = state[0, 4 * s + i]
            dirs[s][4 + i] = state[1, 4 * s + i]
            rel[s][4 + i] = state[2, 4 * s + i]
    for k in range(1, STEPS + 1):
        bf = [{p: dirs[s][p].astype(BF16) for p in range(k - 1, k + 4)} for s in range(2)]
        for s in range(2):
            bf[s][k + 4] = near[4 * s + k - 1]
        for p in range(k, k + 4):
            for s in range(2):
                order = (p - 1, p, p + 1) if s == 0 else (p + 1, p, p - 1)
                v = jnp.concatenate([bf[s][q] for q in order], axis=1)
                r = res[s][p] - times(v, stack[s, p])
                res[s][p] = r
                if k < STEPS:
                    c0, c1 = COEFS[k - 1]
                    dirs[s][p] = c0 * dirs[s][p] + c1 * r
                    if p >= 4:
                        rel[s][p] = rel[s][p] + dirs[s][p]
    totals = []
    for s in range(2):
        total = sums_in[s]
        for i in range(4):
            total = total + res[s][4 + i].astype(BF16).astype(F32)
            edge[4 * s + (i if s == 0 else 3 - i)] = rel[s][4 + i]
        totals.append(total)
    own = info[0] == 0
    keep[...] = jnp.where(own, totals[0], totals[1])
    give[...] = jnp.where(own, totals[1], totals[0]).astype(BF16)


def place_kernel(edge, inner, rel, sems):
    parts = ((edge.at[0:4], rel.at[0:4]), (inner.at[4:28], rel.at[4:28]), (edge.at[4:8], rel.at[28:32]))
    copies = [pltpu.make_async_copy(a, b, sems.at[i]) for i, (a, b) in enumerate(parts)]
    for c in copies:
        c.start()
    for c in copies:
        c.wait()


def spread_kernel(count, a, b, out):
    s = (a[...] + b[...].astype(F32)).astype(BF16)
    for i in range(count):
        out[i] = s


def sum_of(ref):
    parts = [ref[i].astype(F32) for i in range(ref.shape[0])]
    while len(parts) > 1:
        parts = [parts[i] + parts[i + 1] for i in range(0, len(parts), 2)]
    return parts[0]


def merge_kernel(count, got, out):
    s = sum_of(got).astype(BF16)
    for i in range(count):
        out[i] = s


def total_kernel(got, out):
    out[...] = sum_of(got)


def halves(a):
    top = a.astype(BF16)
    return top, (a - top.astype(F32)).astype(BF16)


def map_kernel(restrict, level, inverse, top, rest):
    r = restrict[...].astype(F32) * 2.0**-5
    for c in range(2):
        one = level[c]
        two = exact(one, one)
        four = exact(two, two)
        eight = exact(four, four)
        head = exact(r, two)
        tail = exact(eight, inverse[c * ROWS : (c + 1) * ROWS, :])
        top[c], rest[c] = halves(exact(head, tail))


def mapped(x, top, rest):
    x_top, x_rest = halves(x)
    return times(x_top, top) + (times(x_top, rest) + times(x_rest, top))


def own_kernel(info, mine, top, rest, out):
    c = info[0]
    out[...] = mapped(mine[...], top[c], rest[c])


def solve_kernel(info, part, other, top, rest, out):
    c = 1 - info[0]
    out[...] = part[...] + mapped(other[...], top[c], rest[c])


def shards(right_side, diag_blocks, link_blocks, restrict_map, level_map, coarse_inverse):
    rhs, diag, link = right_side[0], diag_blocks[0], link_blocks[0]
    tile, pack = (VECS, ROWS), (8, ROWS, ROWS)
    half = lax.axis_index("core")
    j = lax.axis_index("x") * 2 + half
    info = jnp.stack([half, (j < 7).astype(jnp.int32)]).astype(jnp.int32)

    to_chip, to_core = call(
        pack_kernel,
        (bf16(pack), bf16(pack)),
        [SMEM] + [HBM] * 3,
        (VMEM, VMEM),
        (info, rhs.reshape(8, ROWS, ROWS), diag, link),
        scratch=[pltpu.SemaphoreType.DMA((6,))],
        mib=53.25,
        cost=(0, 1 << 20),
    )
    across = [(1, 2), (2, 1), (3, 4), (4, 3), (5, 6), (6, 5)]
    swap = [(0, 1), (1, 0)]
    chip = lax.ppermute(to_chip, ("x", "core"), across)
    core = lax.ppermute(to_core, "core", swap)

    rel, state, near, sums = call(
        inner_kernel,
        (f32((TILES,) + tile), f32((3, 8) + tile), bf16((8,) + tile), f32((2,) + tile)),
        [VMEM] * 3,
        (VMEM,) * 4,
        (rhs, diag, link),
        scratch=[
            pltpu.VMEM((TILES,) + tile, F32),
            pltpu.VMEM((TILES,) + tile, F32),
            pltpu.VMEM((2, TILES) + tile, BF16),
            pltpu.VMEM((TILES, 3 * ROWS, ROWS), BF16),
        ],
        mib=24,
        cost=(4 * 10**8, 3 << 20),
    )
    edge, keep, give = call(
        edge_kernel,
        (f32((8,) + tile), f32(tile), bf16(tile)),
        [SMEM] + [VMEM] * 7,
        (VMEM,) * 3,
        (info, chip, core, diag, link, state, near, sums),
        scratch=[pltpu.VMEM((2, 8, 3 * ROWS, ROWS), BF16), pltpu.VMEM((2, 4) + tile, BF16)],
        mib=16,
        cost=(10**8, 1 << 20),
    )

    got = lax.ppermute(give, "core", swap)
    copies = call(
        functools.partial(spread_kernel, 32), bf16((32,) + tile), [VMEM] * 2, VMEM, (keep, got), cost=(0, 1 << 18)
    )
    copies = lax.all_to_all(copies, ("y", "x"), 0, 0, tiled=True)
    copies = call(functools.partial(merge_kernel, 16), bf16((16,) + tile), [VMEM], VMEM, (copies,), cost=(0, 1 << 18))
    copies, restrict_map, edge = lax.optimization_barrier((copies, restrict_map, edge))
    copies = lax.all_to_all(copies, "z", 0, 0, tiled=True)
    top, rest = call(
        map_kernel,
        (bf16((2, ROWS, 2 * ROWS)),) * 2,
        [VMEM] * 3,
        (VMEM,) * 2,
        (restrict_map, level_map, coarse_inverse),
        cost=(4 * 10**8, 1 << 19),
    )
    rel = call(
        place_kernel,
        f32((TILES,) + tile),
        [VMEM, VMEM],
        HBM,
        (edge, rel),
        scratch=[pltpu.SemaphoreType.DMA((3,))],
        cost=(0, 1 << 20),
    )
    mine = call(total_kernel, f32(tile), [VMEM], VMEM, (copies,), cost=(0, 1 << 17))
    mine, top, rest, rel = lax.optimization_barrier((mine, top, rest, rel))
    other = lax.ppermute(mine, "core", swap)
    wide = f32((VECS, 2 * ROWS))
    part = call(own_kernel, wide, [SMEM] + [VMEM] * 3, VMEM, (info, mine, top, rest), cost=(10**7, 1 << 17))
    solved = call(
        solve_kernel, wide, [SMEM] + [VMEM] * 4, VMEM, (info, part, other, top, rest), cost=(10**7, 1 << 17)
    )
    return (rel[None], solved[None, None])


def solution(mesh):
    fine = Mesh(mesh.devices.reshape(8, 16, 4, 2), ("y", "z", "x", "core"))
    big = P(("y", "z"), ("x", "core"), None, None)
    return jax.shard_map(
        shards,
        mesh=fine,
        in_specs=(big, big, big, P(), P(), P()),
        out_specs=(big, big),
        check_vma=False,
    )
```

```python
import functools

import jax
import jax.numpy as jnp
from jax import lax
from jax.experimental import pallas as pl
from jax.experimental.pallas import tpu as pltpu
from jax.sharding import Mesh
from jax.sharding import PartitionSpec as P

TILES = 32
VECS = 32
ROWS = 128
STEPS = 4
HALF = TILES // 2
BF16, F32 = jnp.bfloat16, jnp.float32


def coefficients():
    theta, delta = 2.0, 1.7
    sigma = theta / delta
    rho = 1.0 / sigma
    out = []
    for _ in range(STEPS - 1):
        rho_new = 1.0 / (2.0 * sigma - rho)
        out.append((rho_new * rho, 2.0 * rho_new / delta))
        rho = rho_new
    return out


COEFS = coefficients()
VMEM = pl.BlockSpec(memory_space=pltpu.VMEM)
SMEM = pl.BlockSpec(memory_space=pltpu.SMEM)
HBM = pl.BlockSpec(memory_space=pltpu.HBM)
f32 = functools.partial(jax.ShapeDtypeStruct, dtype=F32)
bf16 = functools.partial(jax.ShapeDtypeStruct, dtype=BF16)


def call(kernel, out_shape, in_specs, out_specs, args, scratch=(), mib=8, cost=(0, 0), **kw):
    return pl.pallas_call(
        kernel,
        out_shape=out_shape,
        in_specs=in_specs,
        out_specs=out_specs,
        scratch_shapes=list(scratch),
        compiler_params=pltpu.CompilerParams(vmem_limit_bytes=int(mib * 2**20)),
        cost_estimate=pl.CostEstimate(flops=cost[0], bytes_accessed=cost[1], transcendentals=0),
        **kw,
    )(*args)


def times(a, b):
    return jnp.dot(a, b, preferred_element_type=F32)


def exact(a, b):
    return jnp.dot(a, b, precision=lax.Precision.HIGHEST, preferred_element_type=F32)


def pack_kernel(info, rhs, diag, link, out, sems):
    c = info[0]
    parts = (
        (rhs.at[pl.ds(7 * c, 1)], out.at[0:1]),
        (diag.at[pl.ds(29 * c, 3)], out.at[1:4]),
        (link.at[pl.ds(28 * c, 4)], out.at[4:8]),
    )
    copies = [pltpu.make_async_copy(src, dst, sems.at[i]) for i, (src, dst) in enumerate(parts)]
    for copy in copies:
        copy.start()
    for copy in copies:
        copy.wait()


def halves(a):
    top = a.astype(BF16)
    return top, (a - top.astype(F32)).astype(BF16)


def rows(i):
    return slice(i * VECS, (i + 1) * VECS)


def inner_kernel(info, rhs, diag, link, rel, state, near, sums, pass_on, resid, direc, dirb, stack):
    for t in range(1, TILES - 1):
        stack[t, 0:ROWS] = link[t - 1]
        stack[t, ROWS : 2 * ROWS] = diag[t]
        stack[t, 2 * ROWS :] = link[t].T
    for t in (0, TILES - 1):
        r = rhs[t].astype(F32)
        resid[t] = r
        direc[t] = r * 0.5
        rel[t] = r * 0.5
    totals = [jnp.zeros((VECS, ROWS), F32) for _ in range(2)]
    for k in range(1, STEPS + 1):
        now, later = (k - 1) % 2, k % 2

        def moved(t):
            return rhs[t] if k == 1 else dirb[now, t]

        near[k - 1] = moved(k) * BF16(0.5) if k == 1 else moved(k)
        near[STEPS + k - 1] = moved(TILES - 1 - k) * BF16(0.5) if k == 1 else moved(TILES - 1 - k)
        for t in range(k, TILES - k):
            v = jnp.concatenate([moved(t - 1), moved(t), moved(t + 1)], axis=1)
            a = times(v, stack[t])
            if k == 1:
                before = rhs[t].astype(F32)
                r = before - 0.5 * a
                d = before * 0.5
                total = d
            else:
                r = resid[t] - a
                d = direc[t] if k < STEPS else None
                total = rel[t] if k < STEPS else None
            if k < STEPS:
                c0, c1 = COEFS[k - 1]
                d = c0 * d + c1 * r
                rel[t] = total + d
                dirb[later, t] = d.astype(BF16)
                resid[t] = r
                if k < STEPS - 1 or t == k or t == TILES - 1 - k:
                    direc[t] = d
            else:
                totals[t // HALF] += r.astype(BF16).astype(F32)
    for i, t in enumerate((0, 1, 2, 3, 31, 30, 29, 28)):
        state[0, i] = resid[t]
        state[1, i] = direc[t]
        state[2, i] = rel[t]
    for c in range(2):
        sums[c] = totals[c]

    def fill(diag0, link0, near0, order, group):
        for i in range(4):
            pass_on[i] = diag[diag0 + i]
        for i in range(5):
            pass_on[4 + i] = link[link0 + i]
        for i in range(4):
            pass_on[9, rows(i), :] = near[near0 + i]
            for which in range(2):
                top, rest = halves(state[which, order[i]])
                pass_on[10 + 2 * which, rows(i), :] = top
                pass_on[11 + 2 * which, rows(i), :] = rest
        top, rest = halves(totals[group])
        for i in range(2):
            pass_on[14, rows(2 * i), :] = top
            pass_on[14, rows(2 * i + 1), :] = rest

    @pl.when(info[0] == 0)
    def _():
        fill(28, 27, 4, (7, 6, 5, 4), 1)

    @pl.when(info[0] != 0)
    def _():
        fill(0, 0, 0, (0, 1, 2, 3), 0)


def sweep(k, span, stack, res, dirs, rel, bf):
    for p in span:
        v = jnp.concatenate([bf[p - 1], bf[p], bf[p + 1]], axis=1)
        r = res[p] - times(v, stack[p])
        res[p] = r
        if k < STEPS:
            c0, c1 = COEFS[k - 1]
            dirs[p] = c0 * dirs[p] + c1 * r
            if p in rel:
                rel[p] = rel[p] + dirs[p]


def total(res, span):
    parts = [res[p].astype(BF16).astype(F32) for p in span]
    return (parts[0] + parts[1]) + (parts[2] + parts[3])


ONE, TWO, THREE = slice(0, ROWS), slice(ROWS, 2 * ROWS), slice(2 * ROWS, 3 * ROWS)


def outer_kernel(info, chip, diag, link, state, near, edge, part, stack, rhs):
    @pl.when(info[0] == 0)
    def _():
        for i in range(4):
            rhs[i] = chip[0, rows(i), :]
        for p in (1, 2, 3):
            stack[p, ONE] = chip[3 + p]
            stack[p, TWO] = chip[p]
            stack[p, THREE] = chip[4 + p].T
        for i in range(4):
            stack[4 + i, ONE] = chip[7] if i == 0 else link[i - 1]
            stack[4 + i, TWO] = diag[i]
            stack[4 + i, THREE] = link[i].T

    @pl.when(info[0] != 0)
    def _():
        last = link[TILES - 1]
        last = jnp.where(info[1] > 0, last, jnp.zeros_like(last))
        for i in range(4):
            rhs[i] = chip[0, rows(3 - i), :]
        for p in (1, 2, 3):
            stack[p, ONE] = chip[7 - p].T
            stack[p, TWO] = chip[4 - p]
            stack[p, THREE] = last if p == 3 else chip[6 - p]
        for i in range(4):
            stack[4 + i, ONE] = link[31 - i].T
            stack[4 + i, TWO] = diag[31 - i]
            stack[4 + i, THREE] = link[30 - i]

    c = info[0]
    res, dirs, rel = {}, {}, {}
    for p in range(8):
        if p < 4:
            res[p] = rhs[p].astype(F32)
            dirs[p] = res[p] * 0.5
        else:
            res[p] = state[0, 4 * c + (p - 4)]
            dirs[p] = state[1, 4 * c + (p - 4)]
            rel[p] = state[2, 4 * c + (p - 4)]
    for k in range(1, STEPS + 1):
        bf = {p: dirs[p].astype(BF16) for p in range(k - 1, k + 4)}
        bf[k + 4] = near[4 * c + (k - 1)]
        sweep(k, range(k, k + 4), stack, res, dirs, rel, bf)
    part[...] = total(res, range(4, 8))

    @pl.when(c == 0)
    def _():
        for i in range(4):
            edge[i] = rel[4 + i]

    @pl.when(c != 0)
    def _():
        for i in range(4):
            edge[3 - i] = rel[4 + i]


def middle_kernel(info, core, diag, link, state, near, sums_in, part, edge, copies, stack, mid, ends):
    def received(block, i):
        return core[block, rows(i), :].astype(F32) + core[block + 1, rows(i), :].astype(F32)

    @pl.when(info[0] == 0)
    def _():
        for i in range(4):
            stack[i, ONE] = link[27 + i]
            stack[i, TWO] = diag[28 + i]
            stack[i, THREE] = link[28 + i].T
            stack[4 + i, ONE] = link[31] if i == 0 else core[3 + i]
            stack[4 + i, TWO] = core[i]
            stack[4 + i, THREE] = core[4 + i].T
            for which in range(2):
                mid[which, i] = state[which, 7 - i]
                mid[which, 4 + i] = received(10 + 2 * which, i)
            mid[2, i] = state[2, 7 - i]
            mid[2, 4 + i] = jnp.zeros((VECS, ROWS), F32)
            ends[0, i] = near[4 + i]
            ends[1, i] = core[9, rows(i), :]

    @pl.when(info[0] != 0)
    def _():
        for i in range(4):
            stack[i, ONE] = core[4 + i]
            stack[i, TWO] = core[i]
            stack[i, THREE] = core[5 + i].T
            stack[4 + i, ONE] = core[8] if i == 0 else link[i - 1]
            stack[4 + i, TWO] = diag[i]
            stack[4 + i, THREE] = link[i].T
            for which in range(2):
                mid[which, i] = received(10 + 2 * which, i)
                mid[which, 4 + i] = state[which, i]
            mid[2, i] = jnp.zeros((VECS, ROWS), F32)
            mid[2, 4 + i] = state[2, i]
            ends[0, i] = core[9, rows(i), :]
            ends[1, i] = near[i]

    c = info[0]
    res, dirs, rel = ({p: mid[which, p] for p in range(8)} for which in range(3))
    for k in range(1, STEPS + 1):
        span = range(4 - k, 4 + k)
        bf = {p: dirs[p].astype(BF16) for p in span}
        bf[3 - k] = ends[0, k - 1]
        bf[4 + k] = ends[1, k - 1]
        sweep(k, span, stack, res, dirs, rel, bf)
    beside = jnp.where(c == 0, total(res, range(4, 8)), total(res, range(4)))
    other = core[14, rows(0), :].astype(F32) + core[14, rows(1), :].astype(F32)
    whole = ((sums_in[c] + other) + (part[...] + beside)).astype(BF16)
    for i in range(copies.shape[0]):
        copies[i] = whole

    @pl.when(c == 0)
    def _():
        for i in range(4):
            edge[i] = rel[i]

    @pl.when(c != 0)
    def _():
        for i in range(4):
            edge[i] = rel[4 + i]


def place_kernel(info, outer, middle, inner, rel, sems):
    c = info[0]
    parts = (
        (outer, rel.at[pl.ds(28 * c, 4)]),
        (inner.at[4:28], rel.at[4:28]),
        (middle, rel.at[pl.ds(28 - 28 * c, 4)]),
    )
    copies = [pltpu.make_async_copy(a, b, sems.at[i]) for i, (a, b) in enumerate(parts)]
    for copy in copies:
        copy.start()
    for copy in copies:
        copy.wait()


def sum_of(ref):
    parts = [ref[i].astype(F32) for i in range(ref.shape[0])]
    while len(parts) > 1:
        parts = [parts[i] + parts[i + 1] for i in range(0, len(parts), 2)]
    return parts[0]


def merge_kernel(count, got, out):
    s = sum_of(got).astype(BF16)
    for i in range(count):
        out[i] = s


def total_kernel(got, out):
    out[...] = sum_of(got)


def map_kernel(restrict, level, inverse, top, rest):
    r = restrict[...].astype(F32) * 2.0**-5
    for c in range(2):
        one = level[c]
        two = exact(one, one)
        four = exact(two, two)
        eight = exact(four, four)
        head = exact(r, two)
        tail = exact(eight, inverse[c * ROWS : (c + 1) * ROWS, :])
        top[c], rest[c] = halves(exact(head, tail))


def mapped(x, top, rest):
    x_top, x_rest = halves(x)
    return times(x_top, top) + (times(x_top, rest) + times(x_rest, top))


def own_kernel(info, mine, top, rest, out):
    c = info[0]
    out[...] = mapped(mine[...], top[c], rest[c])


def solve_kernel(info, part, other, top, rest, out):
    c = 1 - info[0]
    out[...] = part[...] + mapped(other[...], top[c], rest[c])


def shards(right_side, diag_blocks, link_blocks, restrict_map, level_map, coarse_inverse):
    rhs, diag, link = right_side[0], diag_blocks[0], link_blocks[0]
    tile, pack = (VECS, ROWS), (8, ROWS, ROWS)
    half = lax.axis_index("core")
    j = lax.axis_index("x") * 2 + half
    info = jnp.stack([half, (j < 7).astype(jnp.int32)]).astype(jnp.int32)

    to_chip = call(
        pack_kernel,
        bf16(pack),
        [SMEM] + [HBM] * 3,
        VMEM,
        (info, rhs.reshape(8, ROWS, ROWS), diag, link),
        scratch=[pltpu.SemaphoreType.DMA((3,))],
        mib=53.5,
        cost=(0, 1 << 19),
    )
    across = [(1, 2), (2, 1), (3, 4), (4, 3), (5, 6), (6, 5)]
    swap = [(0, 1), (1, 0)]
    to_chip, later = lax.optimization_barrier((to_chip, info))
    chip = lax.ppermute(to_chip, ("x", "core"), across)

    rel, state, near, sums, pass_on = call(
        inner_kernel,
        (
            f32((TILES,) + tile),
            f32((3, 8) + tile),
            bf16((8,) + tile),
            f32((2,) + tile),
            bf16((15, ROWS, ROWS)),
        ),
        [SMEM] + [VMEM] * 3,
        (VMEM,) * 5,
        (later, rhs, diag, link),
        scratch=[
            pltpu.VMEM((TILES,) + tile, F32),
            pltpu.VMEM((TILES,) + tile, F32),
            pltpu.VMEM((2, TILES) + tile, BF16),
            pltpu.VMEM((TILES, 3 * ROWS, ROWS), BF16),
        ],
        mib=24,
        cost=(4 * 10**8, 3 << 20),
    )
    core = lax.ppermute(pass_on, "core", swap)
    outer, part = call(
        outer_kernel,
        (f32((4,) + tile), f32(tile)),
        [SMEM] + [VMEM] * 5,
        (VMEM,) * 2,
        (info, chip, diag, link, state, near),
        scratch=[pltpu.VMEM((8, 3 * ROWS, ROWS), BF16), pltpu.VMEM((4,) + tile, BF16)],
        mib=16,
        cost=(5 * 10**9, 1 << 20),
    )
    middle, copies = call(
        middle_kernel,
        (f32((4,) + tile), bf16((32,) + tile)),
        [SMEM] + [VMEM] * 7,
        (VMEM,) * 2,
        (info, core, diag, link, state, near, sums, part),
        scratch=[
            pltpu.VMEM((8, 3 * ROWS, ROWS), BF16),
            pltpu.VMEM((3, 8) + tile, F32),
            pltpu.VMEM((2, 4) + tile, BF16),
        ],
        mib=16,
        cost=(10**8, 1 << 20),
    )
    copies = lax.all_to_all(copies, ("y", "x"), 0, 0, tiled=True)
    copies = call(functools.partial(merge_kernel, 16), bf16((16,) + tile), [VMEM], VMEM, (copies,), cost=(0, 1 << 18))
    copies, restrict_map, outer = lax.optimization_barrier((copies, restrict_map, outer))
    copies = lax.all_to_all(copies, "z", 0, 0, tiled=True)
    top, rest = call(
        map_kernel,
        (bf16((2, ROWS, 2 * ROWS)),) * 2,
        [VMEM] * 3,
        (VMEM,) * 2,
        (restrict_map, level_map, coarse_inverse),
        cost=(4 * 10**8, 1 << 19),
    )
    rel = call(
        place_kernel,
        f32((TILES,) + tile),
        [SMEM] + [VMEM] * 3,
        HBM,
        (info, outer, middle, rel),
        scratch=[pltpu.SemaphoreType.DMA((3,))],
        cost=(0, 1 << 20),
    )
    mine = call(total_kernel, f32(tile), [VMEM], VMEM, (copies,), cost=(0, 1 << 17))
    mine, top, rest, rel = lax.optimization_barrier((mine, top, rest, rel))
    other = lax.ppermute(mine, "core", swap)
    wide = f32((VECS, 2 * ROWS))
    part = call(own_kernel, wide, [SMEM] + [VMEM] * 3, VMEM, (info, mine, top, rest), cost=(10**7, 1 << 17))
    solved = call(
        solve_kernel, wide, [SMEM] + [VMEM] * 4, VMEM, (info, part, other, top, rest), cost=(10**7, 1 << 17)
    )
    return (rel[None], solved[None, None])


def solution(mesh):
    fine = Mesh(mesh.devices.reshape(8, 16, 4, 2), ("y", "z", "x", "core"))
    big = P(("y", "z"), ("x", "core"), None, None)
    return jax.shard_map(
        shards,
        mesh=fine,
        in_specs=(big, big, big, P(), P(), P()),
        out_specs=(big, big),
        check_vma=False,
    )
```

```python
import functools

import jax
import jax.numpy as jnp
from jax import lax
from jax.experimental import pallas as pl
from jax.experimental.pallas import tpu as pltpu
from jax.sharding import Mesh
from jax.sharding import PartitionSpec as P

TILES = 32
VECS = 32
ROWS = 128
STEPS = 4
HALF = TILES // 2
BF16, F32 = jnp.bfloat16, jnp.float32


def coefficients():
    theta, delta = 2.0, 1.7
    sigma = theta / delta
    rho = 1.0 / sigma
    out = []
    for _ in range(STEPS - 1):
        rho_new = 1.0 / (2.0 * sigma - rho)
        out.append((rho_new * rho, 2.0 * rho_new / delta))
        rho = rho_new
    return out


COEFS = coefficients()
VMEM = pl.BlockSpec(memory_space=pltpu.VMEM)
HBM = pl.BlockSpec(memory_space=pltpu.HBM)
f32 = functools.partial(jax.ShapeDtypeStruct, dtype=F32)
bf16 = functools.partial(jax.ShapeDtypeStruct, dtype=BF16)


def call(kernel, out_shape, in_specs, out_specs, args, scratch=(), mib=8, cost=(0, 0), **kw):
    return pl.pallas_call(
        kernel,
        out_shape=out_shape,
        in_specs=in_specs,
        out_specs=out_specs,
        scratch_shapes=list(scratch),
        compiler_params=pltpu.CompilerParams(vmem_limit_bytes=int(mib * 2**20)),
        cost_estimate=pl.CostEstimate(flops=cost[0], bytes_accessed=cost[1], transcendentals=0),
        **kw,
    )(*args)


def core_index():
    return lax.axis_index("core")


def times(a, b):
    return jnp.dot(a, b, preferred_element_type=F32)


def exact(a, b):
    return jnp.dot(a, b, precision=lax.Precision.HIGHEST, preferred_element_type=F32)


def pack_kernel(rhs, diag, link, out, sems):
    c = core_index()
    parts = (
        (rhs.at[pl.ds(7 * c, 1)], out.at[0:1]),
        (diag.at[pl.ds(29 * c, 3)], out.at[1:4]),
        (link.at[pl.ds(28 * c, 4)], out.at[4:8]),
    )
    copies = [pltpu.make_async_copy(src, dst, sems.at[i]) for i, (src, dst) in enumerate(parts)]
    for copy in copies:
        copy.start()
    for copy in copies:
        copy.wait()


def halves(a):
    top = a.astype(BF16)
    return top, (a - top.astype(F32)).astype(BF16)


def rows(i):
    return slice(i * VECS, (i + 1) * VECS)


def inner_kernel(rhs, diag, link, rel, state, near, sums, pass_on, resid, direc, dirb, stack):
    for t in range(1, TILES - 1):
        stack[t, 0:ROWS] = link[t - 1]
        stack[t, ROWS : 2 * ROWS] = diag[t]
        stack[t, 2 * ROWS :] = link[t].T
    for t in (0, TILES - 1):
        r = rhs[t].astype(F32)
        resid[t] = r
        direc[t] = r * 0.5
        rel[t] = r * 0.5
    totals = [jnp.zeros((VECS, ROWS), F32) for _ in range(2)]
    for k in range(1, STEPS + 1):
        now, later = (k - 1) % 2, k % 2

        def moved(t):
            return rhs[t] if k == 1 else dirb[now, t]

        near[k - 1] = moved(k) * BF16(0.5) if k == 1 else moved(k)
        near[STEPS + k - 1] = moved(TILES - 1 - k) * BF16(0.5) if k == 1 else moved(TILES - 1 - k)
        for t in range(k, TILES - k):
            v = jnp.concatenate([moved(t - 1), moved(t), moved(t + 1)], axis=1)
            a = times(v, stack[t])
            if k == 1:
                before = rhs[t].astype(F32)
                r = before - 0.5 * a
                d = before * 0.5
                total = d
            else:
                r = resid[t] - a
                d = direc[t] if k < STEPS else None
                total = rel[t] if k < STEPS else None
            if k < STEPS:
                c0, c1 = COEFS[k - 1]
                d = c0 * d + c1 * r
                rel[t] = total + d
                dirb[later, t] = d.astype(BF16)
                resid[t] = r
                if k < STEPS - 1 or t == k or t == TILES - 1 - k:
                    direc[t] = d
            else:
                totals[t // HALF] += r.astype(BF16).astype(F32)
    for i, t in enumerate((0, 1, 2, 3, 31, 30, 29, 28)):
        state[0, i] = resid[t]
        state[1, i] = direc[t]
        state[2, i] = rel[t]
    for c in range(2):
        sums[c] = totals[c]

    def fill(diag0, link0, near0, order, group):
        for i in range(4):
            pass_on[i] = diag[diag0 + i]
        for i in range(5):
            pass_on[4 + i] = link[link0 + i]
        for i in range(4):
            pass_on[9, rows(i), :] = near[near0 + i]
            for which in range(2):
                top, rest = halves(state[which, order[i]])
                pass_on[10 + 2 * which, rows(i), :] = top
                pass_on[11 + 2 * which, rows(i), :] = rest
        top, rest = halves(totals[group])
        for i in range(2):
            pass_on[14, rows(2 * i), :] = top
            pass_on[14, rows(2 * i + 1), :] = rest

    @pl.when(core_index() == 0)
    def _():
        fill(28, 27, 4, (7, 6, 5, 4), 1)

    @pl.when(core_index() != 0)
    def _():
        fill(0, 0, 0, (0, 1, 2, 3), 0)


def sweep(k, span, stack, res, dirs, rel, bf):
    for p in span:
        v = jnp.concatenate([bf[p - 1], bf[p], bf[p + 1]], axis=1)
        r = res[p] - times(v, stack[p])
        res[p] = r
        if k < STEPS:
            c0, c1 = COEFS[k - 1]
            dirs[p] = c0 * dirs[p] + c1 * r
            if p in rel:
                rel[p] = rel[p] + dirs[p]


def total(res, span):
    parts = [res[p].astype(BF16).astype(F32) for p in span]
    return (parts[0] + parts[1]) + (parts[2] + parts[3])


ONE, TWO, THREE = slice(0, ROWS), slice(ROWS, 2 * ROWS), slice(2 * ROWS, 3 * ROWS)


def outer_kernel(chip, diag, link, state, near, edge, part, stack, rhs):
    @pl.when(core_index() == 0)
    def _():
        for i in range(4):
            rhs[i] = chip[0, rows(i), :]
        for p in (1, 2, 3):
            stack[p, ONE] = chip[3 + p]
            stack[p, TWO] = chip[p]
            stack[p, THREE] = chip[4 + p].T
        for i in range(4):
            stack[4 + i, ONE] = chip[7] if i == 0 else link[i - 1]
            stack[4 + i, TWO] = diag[i]
            stack[4 + i, THREE] = link[i].T

    @pl.when(core_index() != 0)
    def _():
        last = link[TILES - 1]
        last = jnp.where(lax.axis_index("x") * 2 + core_index() < 7, last, jnp.zeros_like(last))
        for i in range(4):
            rhs[i] = chip[0, rows(3 - i), :]
        for p in (1, 2, 3):
            stack[p, ONE] = chip[7 - p].T
            stack[p, TWO] = chip[4 - p]
            stack[p, THREE] = last if p == 3 else chip[6 - p]
        for i in range(4):
            stack[4 + i, ONE] = link[31 - i].T
            stack[4 + i, TWO] = diag[31 - i]
            stack[4 + i, THREE] = link[30 - i]

    c = core_index()
    res, dirs, rel = {}, {}, {}
    for p in range(8):
        if p < 4:
            res[p] = rhs[p].astype(F32)
            dirs[p] = res[p] * 0.5
        else:
            res[p] = state[0, 4 * c + (p - 4)]
            dirs[p] = state[1, 4 * c + (p - 4)]
            rel[p] = state[2, 4 * c + (p - 4)]
    for k in range(1, STEPS + 1):
        bf = {p: dirs[p].astype(BF16) for p in range(k - 1, k + 4)}
        bf[k + 4] = near[4 * c + (k - 1)]
        sweep(k, range(k, k + 4), stack, res, dirs, rel, bf)
    part[...] = total(res, range(4, 8))

    @pl.when(c == 0)
    def _():
        for i in range(4):
            edge[i] = rel[4 + i]

    @pl.when(c != 0)
    def _():
        for i in range(4):
            edge[3 - i] = rel[4 + i]


def middle_kernel(core, diag, link, state, near, sums_in, part, edge, copies, stack, mid, ends):
    def received(block, i):
        return core[block, rows(i), :].astype(F32) + core[block + 1, rows(i), :].astype(F32)

    @pl.when(core_index() == 0)
    def _():
        for i in range(4):
            stack[i, ONE] = link[27 + i]
            stack[i, TWO] = diag[28 + i]
            stack[i, THREE] = link[28 + i].T
            stack[4 + i, ONE] = link[31] if i == 0 else core[3 + i]
            stack[4 + i, TWO] = core[i]
            stack[4 + i, THREE] = core[4 + i].T
            for which in range(2):
                mid[which, i] = state[which, 7 - i]
                mid[which, 4 + i] = received(10 + 2 * which, i)
            mid[2, i] = state[2, 7 - i]
            mid[2, 4 + i] = jnp.zeros((VECS, ROWS), F32)
            ends[0, i] = near[4 + i]
            ends[1, i] = core[9, rows(i), :]

    @pl.when(core_index() != 0)
    def _():
        for i in range(4):
            stack[i, ONE] = core[4 + i]
            stack[i, TWO] = core[i]
            stack[i, THREE] = core[5 + i].T
            stack[4 + i, ONE] = core[8] if i == 0 else link[i - 1]
            stack[4 + i, TWO] = diag[i]
            stack[4 + i, THREE] = link[i].T
            for which in range(2):
                mid[which, i] = received(10 + 2 * which, i)
                mid[which, 4 + i] = state[which, i]
            mid[2, i] = jnp.zeros((VECS, ROWS), F32)
            mid[2, 4 + i] = state[2, i]
            ends[0, i] = core[9, rows(i), :]
            ends[1, i] = near[i]

    c = core_index()
    res, dirs, rel = ({p: mid[which, p] for p in range(8)} for which in range(3))
    for k in range(1, STEPS + 1):
        span = range(4 - k, 4 + k)
        bf = {p: dirs[p].astype(BF16) for p in span}
        bf[3 - k] = ends[0, k - 1]
        bf[4 + k] = ends[1, k - 1]
        sweep(k, span, stack, res, dirs, rel, bf)
    beside = jnp.where(c == 0, total(res, range(4, 8)), total(res, range(4)))
    other = core[14, rows(0), :].astype(F32) + core[14, rows(1), :].astype(F32)
    whole = ((sums_in[c] + other) + (part[...] + beside)).astype(BF16)
    for i in range(copies.shape[0]):
        copies[i] = whole

    @pl.when(c == 0)
    def _():
        for i in range(4):
            edge[i] = rel[i]

    @pl.when(c != 0)
    def _():
        for i in range(4):
            edge[i] = rel[4 + i]


def place_kernel(outer, middle, inner, rel, sems):
    c = core_index()
    parts = (
        (outer, rel.at[pl.ds(28 * c, 4)]),
        (inner.at[4:28], rel.at[4:28]),
        (middle, rel.at[pl.ds(28 - 28 * c, 4)]),
    )
    copies = [pltpu.make_async_copy(a, b, sems.at[i]) for i, (a, b) in enumerate(parts)]
    for copy in copies:
        copy.start()
    for copy in copies:
        copy.wait()


def sum_of(ref):
    parts = [ref[i].astype(F32) for i in range(ref.shape[0])]
    while len(parts) > 1:
        parts = [parts[i] + parts[i + 1] for i in range(0, len(parts), 2)]
    return parts[0]


def merge_kernel(count, got, out):
    s = sum_of(got).astype(BF16)
    for i in range(count):
        out[i] = s


def total_kernel(got, out):
    out[...] = sum_of(got)


def map_kernel(restrict, level, inverse, top, rest):
    r = restrict[...].astype(F32) * 2.0**-5
    for c in range(2):
        one = level[c]
        two = exact(one, one)
        four = exact(two, two)
        eight = exact(four, four)
        head = exact(r, two)
        tail = exact(eight, inverse[c * ROWS : (c + 1) * ROWS, :])
        top[c], rest[c] = halves(exact(head, tail))


def mapped(x, top, rest):
    x_top, x_rest = halves(x)
    return times(x_top, top) + (times(x_top, rest) + times(x_rest, top))


def own_kernel(mine, top, rest, out):
    c = core_index()
    out[...] = mapped(mine[...], top[c], rest[c])


def solve_kernel(part, other, top, rest, out):
    c = 1 - core_index()
    out[...] = part[...] + mapped(other[...], top[c], rest[c])


def shards(right_side, diag_blocks, link_blocks, restrict_map, level_map, coarse_inverse):
    rhs, diag, link = right_side[0], diag_blocks[0], link_blocks[0]
    tile, pack = (VECS, ROWS), (8, ROWS, ROWS)
    to_chip = call(
        pack_kernel,
        bf16(pack),
        [HBM] * 3,
        VMEM,
        (rhs.reshape(8, ROWS, ROWS), diag, link),
        scratch=[pltpu.SemaphoreType.DMA((3,))],
        mib=53.5,
        cost=(0, 1 << 19),
    )
    across = [(1, 2), (2, 1), (3, 4), (4, 3), (5, 6), (6, 5)]
    swap = [(0, 1), (1, 0)]
    to_chip, later = lax.optimization_barrier((to_chip, rhs))
    chip = lax.ppermute(to_chip, ("x", "core"), across)

    rel, state, near, sums, pass_on = call(
        inner_kernel,
        (
            f32((TILES,) + tile),
            f32((3, 8) + tile),
            bf16((8,) + tile),
            f32((2,) + tile),
            bf16((15, ROWS, ROWS)),
        ),
        [VMEM] * 3,
        (VMEM,) * 5,
        (later, diag, link),
        scratch=[
            pltpu.VMEM((TILES,) + tile, F32),
            pltpu.VMEM((TILES,) + tile, F32),
            pltpu.VMEM((2, TILES) + tile, BF16),
            pltpu.VMEM((TILES, 3 * ROWS, ROWS), BF16),
        ],
        mib=24,
        cost=(4 * 10**8, 3 << 20),
    )
    core = lax.ppermute(pass_on, "core", swap)
    outer, part = call(
        outer_kernel,
        (f32((4,) + tile), f32(tile)),
        [VMEM] * 5,
        (VMEM,) * 2,
        (chip, diag, link, state, near),
        scratch=[pltpu.VMEM((8, 3 * ROWS, ROWS), BF16), pltpu.VMEM((4,) + tile, BF16)],
        mib=16,
        cost=(5 * 10**9, 1 << 20),
    )
    middle, copies = call(
        middle_kernel,
        (f32((4,) + tile), bf16((32,) + tile)),
        [VMEM] * 7,
        (VMEM,) * 2,
        (core, diag, link, state, near, sums, part),
        scratch=[
            pltpu.VMEM((8, 3 * ROWS, ROWS), BF16),
            pltpu.VMEM((3, 8) + tile, F32),
            pltpu.VMEM((2, 4) + tile, BF16),
        ],
        mib=16,
        cost=(10**8, 1 << 20),
    )
    copies = lax.all_to_all(copies, ("y", "x"), 0, 0, tiled=True)
    copies = call(functools.partial(merge_kernel, 16), bf16((16,) + tile), [VMEM], VMEM, (copies,), cost=(0, 1 << 18))
    copies, restrict_map, outer = lax.optimization_barrier((copies, restrict_map, outer))
    copies = lax.all_to_all(copies, "z", 0, 0, tiled=True)
    top, rest = call(
        map_kernel,
        (bf16((2, ROWS, 2 * ROWS)),) * 2,
        [VMEM] * 3,
        (VMEM,) * 2,
        (restrict_map, level_map, coarse_inverse),
        cost=(4 * 10**8, 1 << 19),
    )
    rel = call(
        place_kernel,
        f32((TILES,) + tile),
        [VMEM] * 3,
        HBM,
        (outer, middle, rel),
        scratch=[pltpu.SemaphoreType.DMA((3,))],
        cost=(0, 1 << 20),
    )
    mine = call(total_kernel, f32(tile), [VMEM], VMEM, (copies,), cost=(0, 1 << 17))
    mine, top, rest, rel = lax.optimization_barrier((mine, top, rest, rel))
    other = lax.ppermute(mine, "core", swap)
    wide = f32((VECS, 2 * ROWS))
    part = call(own_kernel, wide, [VMEM] * 3, VMEM, (mine, top, rest), cost=(10**7, 1 << 17))
    solved = call(
        solve_kernel, wide, [VMEM] * 4, VMEM, (part, other, top, rest), cost=(10**7, 1 << 17)
    )
    return (rel[None], solved[None, None])


def solution(mesh):
    fine = Mesh(mesh.devices.reshape(8, 16, 4, 2), ("y", "z", "x", "core"))
    big = P(("y", "z"), ("x", "core"), None, None)
    return jax.shard_map(
        shards,
        mesh=fine,
        in_specs=(big, big, big, P(), P(), P()),
        out_specs=(big, big),
        check_vma=False,
    )
```

```python
import functools

import jax
import jax.numpy as jnp
from jax import lax
from jax.experimental import pallas as pl
from jax.experimental.pallas import tpu as pltpu
from jax.sharding import Mesh
from jax.sharding import PartitionSpec as P

TILES = 32
VECS = 32
ROWS = 128
STEPS = 4
HALF = TILES // 2
BF16, F32 = jnp.bfloat16, jnp.float32


def coefficients():
    theta, delta = 2.0, 1.7
    sigma = theta / delta
    rho = 1.0 / sigma
    out = []
    for _ in range(STEPS - 1):
        rho_new = 1.0 / (2.0 * sigma - rho)
        out.append((rho_new * rho, 2.0 * rho_new / delta))
        rho = rho_new
    return out


COEFS = coefficients()
PLANE = [(4 + y) % 8 * 4 + (2 + x) % 4 for y in range(8) for x in range(4)]
COLUMN = [(12 + z) % 16 for z in range(16)]
VMEM = pl.BlockSpec(memory_space=pltpu.VMEM)
HBM = pl.BlockSpec(memory_space=pltpu.HBM)
f32 = functools.partial(jax.ShapeDtypeStruct, dtype=F32)
bf16 = functools.partial(jax.ShapeDtypeStruct, dtype=BF16)


def call(kernel, out_shape, in_specs, out_specs, args, scratch=(), mib=8, cost=(0, 0), **kw):
    return pl.pallas_call(
        kernel,
        out_shape=out_shape,
        in_specs=in_specs,
        out_specs=out_specs,
        scratch_shapes=list(scratch),
        compiler_params=pltpu.CompilerParams(vmem_limit_bytes=int(mib * 2**20)),
        cost_estimate=pl.CostEstimate(flops=cost[0], bytes_accessed=cost[1], transcendentals=0),
        **kw,
    )(*args)


def core_index():
    return lax.axis_index("core")


def times(a, b):
    return jnp.dot(a, b, preferred_element_type=F32)


def exact(a, b):
    return jnp.dot(a, b, precision=lax.Precision.HIGHEST, preferred_element_type=F32)


def pack_kernel(rhs, diag, link, out, sems):
    c = core_index()
    parts = (
        (rhs.at[pl.ds(7 * c, 1)], out.at[0:1]),
        (diag.at[pl.ds(29 * c, 3)], out.at[1:4]),
        (link.at[pl.ds(28 * c, 4)], out.at[4:8]),
    )
    copies = [pltpu.make_async_copy(src, dst, sems.at[i]) for i, (src, dst) in enumerate(parts)]
    for copy in copies:
        copy.start()
    for copy in copies:
        copy.wait()


def halves(a):
    top = a.astype(BF16)
    return top, (a - top.astype(F32)).astype(BF16)


def rows(i):
    return slice(i * VECS, (i + 1) * VECS)


def inner_kernel(rhs, diag, link, rel, state, near, sums, pass_on, resid, direc, dirb, stack):
    for t in range(1, TILES - 1):
        stack[t, 0:ROWS] = link[t - 1]
        stack[t, ROWS : 2 * ROWS] = diag[t]
        stack[t, 2 * ROWS :] = link[t].T
    for t in (0, TILES - 1):
        r = rhs[t].astype(F32)
        resid[t] = r
        direc[t] = r * 0.5
        rel[t] = r * 0.5
    totals = [jnp.zeros((VECS, ROWS), F32) for _ in range(2)]
    for k in range(1, STEPS + 1):
        now, later = (k - 1) % 2, k % 2

        def moved(t):
            return rhs[t] if k == 1 else dirb[now, t]

        near[k - 1] = moved(k) * BF16(0.5) if k == 1 else moved(k)
        near[STEPS + k - 1] = moved(TILES - 1 - k) * BF16(0.5) if k == 1 else moved(TILES - 1 - k)
        for t in range(k, TILES - k):
            v = jnp.concatenate([moved(t - 1), moved(t), moved(t + 1)], axis=1)
            a = times(v, stack[t])
            if k == 1:
                before = rhs[t].astype(F32)
                r = before - 0.5 * a
                d = before * 0.5
                total = d
            else:
                r = resid[t] - a
                d = direc[t] if k < STEPS else None
                total = rel[t] if k < STEPS else None
            if k < STEPS:
                c0, c1 = COEFS[k - 1]
                d = c0 * d + c1 * r
                rel[t] = total + d
                dirb[later, t] = d.astype(BF16)
                resid[t] = r
                if k < STEPS - 1 or t == k or t == TILES - 1 - k:
                    direc[t] = d
            else:
                totals[t // HALF] += r.astype(BF16).astype(F32)
    for i, t in enumerate((0, 1, 2, 3, 31, 30, 29, 28)):
        state[0, i] = resid[t]
        state[1, i] = direc[t]
        state[2, i] = rel[t]
    for c in range(2):
        sums[c] = totals[c]

    def fill(diag0, link0, near0, order, group):
        for i in range(4):
            pass_on[i] = diag[diag0 + i]
        for i in range(5):
            pass_on[4 + i] = link[link0 + i]
        for i in range(4):
            pass_on[9, rows(i), :] = near[near0 + i]
            for which in range(2):
                top, rest = halves(state[which, order[i]])
                pass_on[10 + 2 * which, rows(i), :] = top
                pass_on[11 + 2 * which, rows(i), :] = rest
        top, rest = halves(totals[group])
        for i in range(2):
            pass_on[14, rows(2 * i), :] = top
            pass_on[14, rows(2 * i + 1), :] = rest

    @pl.when(core_index() == 0)
    def _():
        fill(28, 27, 4, (7, 6, 5, 4), 1)

    @pl.when(core_index() != 0)
    def _():
        fill(0, 0, 0, (0, 1, 2, 3), 0)


def sweep(k, span, stack, res, dirs, rel, bf):
    for p in span:
        v = jnp.concatenate([bf[p - 1], bf[p], bf[p + 1]], axis=1)
        r = res[p] - times(v, stack[p])
        res[p] = r
        if k < STEPS:
            c0, c1 = COEFS[k - 1]
            dirs[p] = c0 * dirs[p] + c1 * r
            if p in rel:
                rel[p] = rel[p] + dirs[p]


def total(res, span):
    parts = [res[p].astype(BF16).astype(F32) for p in span]
    return (parts[0] + parts[1]) + (parts[2] + parts[3])


ONE, TWO, THREE = slice(0, ROWS), slice(ROWS, 2 * ROWS), slice(2 * ROWS, 3 * ROWS)


def outer_kernel(chip, diag, link, state, near, edge, part, stack, rhs):
    @pl.when(core_index() == 0)
    def _():
        for i in range(4):
            rhs[i] = chip[0, rows(i), :]
        for p in (1, 2, 3):
            stack[p, ONE] = chip[3 + p]
            stack[p, TWO] = chip[p]
            stack[p, THREE] = chip[4 + p].T
        for i in range(4):
            stack[4 + i, ONE] = chip[7] if i == 0 else link[i - 1]
            stack[4 + i, TWO] = diag[i]
            stack[4 + i, THREE] = link[i].T

    @pl.when(core_index() != 0)
    def _():
        last = link[TILES - 1]
        last = jnp.where(lax.axis_index("x") * 2 + core_index() < 7, last, jnp.zeros_like(last))
        for i in range(4):
            rhs[i] = chip[0, rows(3 - i), :]
        for p in (1, 2, 3):
            stack[p, ONE] = chip[7 - p].T
            stack[p, TWO] = chip[4 - p]
            stack[p, THREE] = last if p == 3 else chip[6 - p]
        for i in range(4):
            stack[4 + i, ONE] = link[31 - i].T
            stack[4 + i, TWO] = diag[31 - i]
            stack[4 + i, THREE] = link[30 - i]

    c = core_index()
    res, dirs, rel = {}, {}, {}
    for p in range(8):
        if p < 4:
            res[p] = rhs[p].astype(F32)
            dirs[p] = res[p] * 0.5
        else:
            res[p] = state[0, 4 * c + (p - 4)]
            dirs[p] = state[1, 4 * c + (p - 4)]
            rel[p] = state[2, 4 * c + (p - 4)]
    for k in range(1, STEPS + 1):
        bf = {p: dirs[p].astype(BF16) for p in range(k - 1, k + 4)}
        bf[k + 4] = near[4 * c + (k - 1)]
        sweep(k, range(k, k + 4), stack, res, dirs, rel, bf)
    part[...] = total(res, range(4, 8))

    @pl.when(c == 0)
    def _():
        for i in range(4):
            edge[i] = rel[4 + i]

    @pl.when(c != 0)
    def _():
        for i in range(4):
            edge[3 - i] = rel[4 + i]


def middle_kernel(core, diag, link, state, near, sums_in, part, edge, copies, stack, mid, ends):
    def received(block, i):
        return core[block, rows(i), :].astype(F32) + core[block + 1, rows(i), :].astype(F32)

    @pl.when(core_index() == 0)
    def _():
        for i in range(4):
            stack[i, ONE] = link[27 + i]
            stack[i, TWO] = diag[28 + i]
            stack[i, THREE] = link[28 + i].T
            stack[4 + i, ONE] = link[31] if i == 0 else core[3 + i]
            stack[4 + i, TWO] = core[i]
            stack[4 + i, THREE] = core[4 + i].T
            for which in range(2):
                mid[which, i] = state[which, 7 - i]
                mid[which, 4 + i] = received(10 + 2 * which, i)
            mid[2, i] = state[2, 7 - i]
            mid[2, 4 + i] = jnp.zeros((VECS, ROWS), F32)
            ends[0, i] = near[4 + i]
            ends[1, i] = core[9, rows(i), :]

    @pl.when(core_index() != 0)
    def _():
        for i in range(4):
            stack[i, ONE] = core[4 + i]
            stack[i, TWO] = core[i]
            stack[i, THREE] = core[5 + i].T
            stack[4 + i, ONE] = core[8] if i == 0 else link[i - 1]
            stack[4 + i, TWO] = diag[i]
            stack[4 + i, THREE] = link[i].T
            for which in range(2):
                mid[which, i] = received(10 + 2 * which, i)
                mid[which, 4 + i] = state[which, i]
            mid[2, i] = jnp.zeros((VECS, ROWS), F32)
            mid[2, 4 + i] = state[2, i]
            ends[0, i] = core[9, rows(i), :]
            ends[1, i] = near[i]

    c = core_index()
    res, dirs, rel = ({p: mid[which, p] for p in range(8)} for which in range(3))
    for k in range(1, STEPS + 1):
        span = range(4 - k, 4 + k)
        bf = {p: dirs[p].astype(BF16) for p in span}
        bf[3 - k] = ends[0, k - 1]
        bf[4 + k] = ends[1, k - 1]
        sweep(k, span, stack, res, dirs, rel, bf)
    beside = jnp.where(c == 0, total(res, range(4, 8)), total(res, range(4)))
    other = core[14, rows(0), :].astype(F32) + core[14, rows(1), :].astype(F32)
    whole = ((sums_in[c] + other) + (part[...] + beside)).astype(BF16)
    for i in range(copies.shape[0]):
        copies[i] = whole

    @pl.when(c == 0)
    def _():
        for i in range(4):
            edge[i] = rel[i]

    @pl.when(c != 0)
    def _():
        for i in range(4):
            edge[i] = rel[4 + i]


def place_kernel(outer, middle, inner, rel, sems):
    c = core_index()
    parts = (
        (outer, rel.at[pl.ds(28 * c, 4)]),
        (inner.at[4:28], rel.at[4:28]),
        (middle, rel.at[pl.ds(28 - 28 * c, 4)]),
    )
    copies = [pltpu.make_async_copy(a, b, sems.at[i]) for i, (a, b) in enumerate(parts)]
    for copy in copies:
        copy.start()
    for copy in copies:
        copy.wait()


def sum_of(ref):
    parts = [ref[i].astype(F32) for i in range(ref.shape[0])]
    while len(parts) > 1:
        parts = [parts[i] + parts[i + 1] for i in range(0, len(parts), 2)]
    return parts[0]


def merge_kernel(count, got, out):
    s = sum_of(got).astype(BF16)
    for i in range(count):
        out[i] = s


def total_kernel(got, out):
    out[...] = sum_of(got)


def map_kernel(restrict, level, inverse, top, rest):
    r = restrict[...].astype(F32) * 2.0**-5
    for c in range(2):
        one = level[c]
        two = exact(one, one)
        four = exact(two, two)
        eight = exact(four, four)
        head = exact(r, two)
        tail = exact(eight, inverse[c * ROWS : (c + 1) * ROWS, :])
        top[c], rest[c] = halves(exact(head, tail))


def mapped(x, top, rest):
    x_top, x_rest = halves(x)
    return times(x_top, top) + (times(x_top, rest) + times(x_rest, top))


def own_kernel(mine, top, rest, out):
    c = core_index()
    out[...] = mapped(mine[...], top[c], rest[c])


def solve_kernel(part, other, top, rest, out):
    c = 1 - core_index()
    out[...] = part[...] + mapped(other[...], top[c], rest[c])


def shards(right_side, diag_blocks, link_blocks, restrict_map, level_map, coarse_inverse):
    rhs, diag, link = right_side[0], diag_blocks[0], link_blocks[0]
    tile, pack = (VECS, ROWS), (8, ROWS, ROWS)
    to_chip = call(
        pack_kernel,
        bf16(pack),
        [HBM] * 3,
        VMEM,
        (rhs.reshape(8, ROWS, ROWS), diag, link),
        scratch=[pltpu.SemaphoreType.DMA((3,))],
        mib=53.5,
        cost=(0, 1 << 19),
    )
    across = [(1, 2), (2, 1), (3, 4), (4, 3), (5, 6), (6, 5)]
    swap = [(0, 1), (1, 0)]
    to_chip, later = lax.optimization_barrier((to_chip, rhs))
    chip = lax.ppermute(to_chip, ("x", "core"), across)

    rel, state, near, sums, pass_on = call(
        inner_kernel,
        (
            f32((TILES,) + tile),
            f32((3, 8) + tile),
            bf16((8,) + tile),
            f32((2,) + tile),
            bf16((15, ROWS, ROWS)),
        ),
        [VMEM] * 3,
        (VMEM,) * 5,
        (later, diag, link),
        scratch=[
            pltpu.VMEM((TILES,) + tile, F32),
            pltpu.VMEM((TILES,) + tile, F32),
            pltpu.VMEM((2, TILES) + tile, BF16),
            pltpu.VMEM((TILES, 3 * ROWS, ROWS), BF16),
        ],
        mib=24,
        cost=(4 * 10**8, 3 << 20),
    )
    core = lax.ppermute(pass_on, "core", swap)
    outer, part = call(
        outer_kernel,
        (f32((4,) + tile), f32(tile)),
        [VMEM] * 5,
        (VMEM,) * 2,
        (chip, diag, link, state, near),
        scratch=[pltpu.VMEM((8, 3 * ROWS, ROWS), BF16), pltpu.VMEM((4,) + tile, BF16)],
        mib=16,
        cost=(5 * 10**9, 1 << 20),
    )
    middle, copies = call(
        middle_kernel,
        (f32((4,) + tile), bf16((32,) + tile)),
        [VMEM] * 7,
        (VMEM,) * 2,
        (core, diag, link, state, near, sums, part),
        scratch=[
            pltpu.VMEM((8, 3 * ROWS, ROWS), BF16),
            pltpu.VMEM((3, 8) + tile, F32),
            pltpu.VMEM((2, 4) + tile, BF16),
        ],
        mib=16,
        cost=(10**8, 1 << 20),
    )
    copies = lax.all_to_all(copies, ("y", "x"), 0, 0, axis_index_groups=[PLANE], tiled=True)
    copies = call(functools.partial(merge_kernel, 16), bf16((16,) + tile), [VMEM], VMEM, (copies,), cost=(0, 1 << 18))
    copies, restrict_map, outer = lax.optimization_barrier((copies, restrict_map, outer))
    copies = lax.all_to_all(copies, "z", 0, 0, axis_index_groups=[COLUMN], tiled=True)
    top, rest = call(
        map_kernel,
        (bf16((2, ROWS, 2 * ROWS)),) * 2,
        [VMEM] * 3,
        (VMEM,) * 2,
        (restrict_map, level_map, coarse_inverse),
        cost=(4 * 10**8, 1 << 19),
    )
    rel = call(
        place_kernel,
        f32((TILES,) + tile),
        [VMEM] * 3,
        HBM,
        (outer, middle, rel),
        scratch=[pltpu.SemaphoreType.DMA((3,))],
        cost=(0, 1 << 20),
    )
    mine = call(total_kernel, f32(tile), [VMEM], VMEM, (copies,), cost=(0, 1 << 17))
    mine, top, rest, rel = lax.optimization_barrier((mine, top, rest, rel))
    other = lax.ppermute(mine, "core", swap)
    wide = f32((VECS, 2 * ROWS))
    part = call(own_kernel, wide, [VMEM] * 3, VMEM, (mine, top, rest), cost=(10**7, 1 << 17))
    solved = call(
        solve_kernel, wide, [VMEM] * 4, VMEM, (part, other, top, rest), cost=(10**7, 1 << 17)
    )
    return (rel[None], solved[None, None])


def solution(mesh):
    fine = Mesh(mesh.devices.reshape(8, 16, 4, 2), ("y", "z", "x", "core"))
    big = P(("y", "z"), ("x", "core"), None, None)
    return jax.shard_map(
        shards,
        mesh=fine,
        in_specs=(big, big, big, P(), P(), P()),
        out_specs=(big, big),
        check_vma=False,
    )
```

```python
import functools

import jax
import jax.numpy as jnp
from jax import lax
from jax.experimental import pallas as pl
from jax.experimental.pallas import tpu as pltpu
from jax.sharding import Mesh
from jax.sharding import PartitionSpec as P

TILES = 32
VECS = 32
ROWS = 128
STEPS = 4
EARLY = 8
HALF = TILES // 2
BF16, F32 = jnp.bfloat16, jnp.float32


def coefficients():
    theta, delta = 2.0, 1.7
    sigma = theta / delta
    rho = 1.0 / sigma
    out = []
    for _ in range(STEPS - 1):
        rho_new = 1.0 / (2.0 * sigma - rho)
        out.append((rho_new * rho, 2.0 * rho_new / delta))
        rho = rho_new
    return out


COEFS = coefficients()
PLANE = [18] + [4 * y + x for y in (0, 1, 7, 2, 6, 3, 5, 4) for x in range(4) if (y, x) != (4, 2)]
COLUMN = [12, 0, 1, 2, 3, 4, 5, 6, 7, 15, 14, 13, 11, 10, 9, 8]
VMEM = pl.BlockSpec(memory_space=pltpu.VMEM)
HBM = pl.BlockSpec(memory_space=pltpu.HBM)
f32 = functools.partial(jax.ShapeDtypeStruct, dtype=F32)
bf16 = functools.partial(jax.ShapeDtypeStruct, dtype=BF16)


def call(kernel, out_shape, in_specs, out_specs, args, scratch=(), mib=8, cost=(0, 0), **kw):
    return pl.pallas_call(
        kernel,
        out_shape=out_shape,
        in_specs=in_specs,
        out_specs=out_specs,
        scratch_shapes=list(scratch),
        compiler_params=pltpu.CompilerParams(vmem_limit_bytes=int(mib * 2**20)),
        cost_estimate=pl.CostEstimate(flops=cost[0], bytes_accessed=cost[1], transcendentals=0),
        **kw,
    )(*args)


def core_index():
    return lax.axis_index("core")


def times(a, b):
    return jnp.dot(a, b, preferred_element_type=F32)


def exact(a, b):
    return jnp.dot(a, b, precision=lax.Precision.HIGHEST, preferred_element_type=F32)


def pack_kernel(rhs, diag, link, out, sems):
    c = core_index()
    parts = (
        (rhs.at[pl.ds(7 * c, 1)], out.at[0:1]),
        (diag.at[pl.ds(29 * c, 3)], out.at[1:4]),
        (link.at[pl.ds(28 * c, 4)], out.at[4:8]),
    )
    copies = [pltpu.make_async_copy(src, dst, sems.at[i]) for i, (src, dst) in enumerate(parts)]
    for copy in copies:
        copy.start()
    for copy in copies:
        copy.wait()


def halves(a):
    top = a.astype(BF16)
    return top, (a - top.astype(F32)).astype(BF16)


def rows(i):
    return slice(i * VECS, (i + 1) * VECS)


def inner_kernel(rhs, diag, link, rel, state, near, sums, pass_on, resid, direc, dirb, stack):
    for t in range(1, TILES - 1):
        stack[t, 0:ROWS] = link[t - 1]
        stack[t, ROWS : 2 * ROWS] = diag[t]
        stack[t, 2 * ROWS :] = link[t].T
    for t in (0, TILES - 1):
        r = rhs[t].astype(F32)
        resid[t] = r
        direc[t] = r * 0.5
        rel[t] = r * 0.5
    totals = [jnp.zeros((VECS, ROWS), F32) for _ in range(2)]
    for k in range(1, STEPS + 1):
        now, later = (k - 1) % 2, k % 2

        def moved(t):
            return rhs[t] if k == 1 else dirb[now, t]

        near[k - 1] = moved(k) * BF16(0.5) if k == 1 else moved(k)
        near[STEPS + k - 1] = moved(TILES - 1 - k) * BF16(0.5) if k == 1 else moved(TILES - 1 - k)
        for t in range(k, TILES - k):
            v = jnp.concatenate([moved(t - 1), moved(t), moved(t + 1)], axis=1)
            a = times(v, stack[t])
            if k == 1:
                before = rhs[t].astype(F32)
                r = before - 0.5 * a
                d = before * 0.5
                total = d
            else:
                r = resid[t] - a
                d = direc[t] if k < STEPS else None
                total = rel[t] if k < STEPS else None
            if k < STEPS:
                c0, c1 = COEFS[k - 1]
                d = c0 * d + c1 * r
                rel[t] = total + d
                dirb[later, t] = d.astype(BF16)
                resid[t] = r
                if k < STEPS - 1 or t == k or t == TILES - 1 - k:
                    direc[t] = d
            else:
                totals[t // HALF] += r.astype(BF16).astype(F32)
    for i, t in enumerate((0, 1, 2, 3, 31, 30, 29, 28)):
        state[0, i] = resid[t]
        state[1, i] = direc[t]
        state[2, i] = rel[t]
    for c in range(2):
        sums[c] = totals[c]

    def fill(diag0, link0, near0, order, group):
        for i in range(4):
            pass_on[i] = diag[diag0 + i]
        for i in range(5):
            pass_on[4 + i] = link[link0 + i]
        for i in range(4):
            pass_on[9, rows(i), :] = near[near0 + i]
            for which in range(2):
                top, rest = halves(state[which, order[i]])
                pass_on[10 + 2 * which, rows(i), :] = top
                pass_on[11 + 2 * which, rows(i), :] = rest
        top, rest = halves(totals[group])
        for i in range(2):
            pass_on[14, rows(2 * i), :] = top
            pass_on[14, rows(2 * i + 1), :] = rest

    @pl.when(core_index() == 0)
    def _():
        fill(28, 27, 4, (7, 6, 5, 4), 1)

    @pl.when(core_index() != 0)
    def _():
        fill(0, 0, 0, (0, 1, 2, 3), 0)


def sweep(k, span, stack, res, dirs, rel, bf):
    for p in span:
        v = jnp.concatenate([bf[p - 1], bf[p], bf[p + 1]], axis=1)
        r = res[p] - times(v, stack[p])
        res[p] = r
        if k < STEPS:
            c0, c1 = COEFS[k - 1]
            dirs[p] = c0 * dirs[p] + c1 * r
            if p in rel:
                rel[p] = rel[p] + dirs[p]


def total(res, span):
    parts = [res[p].astype(BF16).astype(F32) for p in span]
    return (parts[0] + parts[1]) + (parts[2] + parts[3])


ONE, TWO, THREE = slice(0, ROWS), slice(ROWS, 2 * ROWS), slice(2 * ROWS, 3 * ROWS)


def outer_kernel(chip, diag, link, state, near, restrict, level, inverse, edge, part, stack, rhs):
    @pl.when(core_index() == 0)
    def _():
        for i in range(4):
            rhs[i] = chip[0, rows(i), :]
        for p in (1, 2, 3):
            stack[p, ONE] = chip[3 + p]
            stack[p, TWO] = chip[p]
            stack[p, THREE] = chip[4 + p].T
        for i in range(4):
            stack[4 + i, ONE] = chip[7] if i == 0 else link[i - 1]
            stack[4 + i, TWO] = diag[i]
            stack[4 + i, THREE] = link[i].T

    @pl.when(core_index() != 0)
    def _():
        last = link[TILES - 1]
        last = jnp.where(lax.axis_index("x") * 2 + core_index() < 7, last, jnp.zeros_like(last))
        for i in range(4):
            rhs[i] = chip[0, rows(3 - i), :]
        for p in (1, 2, 3):
            stack[p, ONE] = chip[7 - p].T
            stack[p, TWO] = chip[4 - p]
            stack[p, THREE] = last if p == 3 else chip[6 - p]
        for i in range(4):
            stack[4 + i, ONE] = link[31 - i].T
            stack[4 + i, TWO] = diag[31 - i]
            stack[4 + i, THREE] = link[30 - i]

    c = core_index()
    res, dirs, rel = {}, {}, {}
    for p in range(8):
        if p < 4:
            res[p] = rhs[p].astype(F32)
            dirs[p] = res[p] * 0.5
        else:
            res[p] = state[0, 4 * c + (p - 4)]
            dirs[p] = state[1, 4 * c + (p - 4)]
            rel[p] = state[2, 4 * c + (p - 4)]
    for k in range(1, STEPS + 1):
        bf = {p: dirs[p].astype(BF16) for p in range(k - 1, k + 4)}
        bf[k + 4] = near[4 * c + (k - 1)]
        sweep(k, range(k, k + 4), stack, res, dirs, rel, bf)
    part[...] = total(res, range(4, 8))

    @pl.when(c == 0)
    def _():
        for i in range(4):
            edge[i] = rel[4 + i]

    @pl.when(c != 0)
    def _():
        for i in range(4):
            edge[3 - i] = rel[4 + i]


def middle_kernel(core, diag, link, state, near, sums_in, part, edge, copies, stack, mid, ends):
    def received(block, i):
        return core[block, rows(i), :].astype(F32) + core[block + 1, rows(i), :].astype(F32)

    @pl.when(core_index() == 0)
    def _():
        for i in range(4):
            stack[i, ONE] = link[27 + i]
            stack[i, TWO] = diag[28 + i]
            stack[i, THREE] = link[28 + i].T
            stack[4 + i, ONE] = link[31] if i == 0 else core[3 + i]
            stack[4 + i, TWO] = core[i]
            stack[4 + i, THREE] = core[4 + i].T
            for which in range(2):
                mid[which, i] = state[which, 7 - i]
                mid[which, 4 + i] = received(10 + 2 * which, i)
            mid[2, i] = state[2, 7 - i]
            mid[2, 4 + i] = jnp.zeros((VECS, ROWS), F32)
            ends[0, i] = near[4 + i]
            ends[1, i] = core[9, rows(i), :]

    @pl.when(core_index() != 0)
    def _():
        for i in range(4):
            stack[i, ONE] = core[4 + i]
            stack[i, TWO] = core[i]
            stack[i, THREE] = core[5 + i].T
            stack[4 + i, ONE] = core[8] if i == 0 else link[i - 1]
            stack[4 + i, TWO] = diag[i]
            stack[4 + i, THREE] = link[i].T
            for which in range(2):
                mid[which, i] = received(10 + 2 * which, i)
                mid[which, 4 + i] = state[which, i]
            mid[2, i] = jnp.zeros((VECS, ROWS), F32)
            mid[2, 4 + i] = state[2, i]
            ends[0, i] = core[9, rows(i), :]
            ends[1, i] = near[i]

    c = core_index()
    res, dirs, rel = ({p: mid[which, p] for p in range(8)} for which in range(3))
    for k in range(1, STEPS + 1):
        span = range(4 - k, 4 + k)
        bf = {p: dirs[p].astype(BF16) for p in span}
        bf[3 - k] = ends[0, k - 1]
        bf[4 + k] = ends[1, k - 1]
        sweep(k, span, stack, res, dirs, rel, bf)
    beside = jnp.where(c == 0, total(res, range(4, 8)), total(res, range(4)))
    other = core[14, rows(0), :].astype(F32) + core[14, rows(1), :].astype(F32)
    whole = ((sums_in[c] + other) + (part[...] + beside)).astype(BF16)
    for i in range(copies.shape[0]):
        copies[i] = whole

    @pl.when(c == 0)
    def _():
        for i in range(4):
            edge[i] = rel[i]

    @pl.when(c != 0)
    def _():
        for i in range(4):
            edge[i] = rel[4 + i]


def place_tiles(outer, middle, inner, rel, sems):
    c = core_index()
    parts = (
        (outer, rel.at[pl.ds(28 * c, 4)]),
        (inner.at[4:28], rel.at[4:28]),
        (middle, rel.at[pl.ds(28 - 28 * c, 4)]),
    )
    copies = [pltpu.make_async_copy(a, b, sems.at[i]) for i, (a, b) in enumerate(parts)]
    for copy in copies:
        copy.start()
    for copy in copies:
        copy.wait()


def sum_of(ref):
    parts = [ref[i].astype(F32) for i in range(ref.shape[0])]
    while len(parts) > 1:
        parts = [parts[i] + parts[i + 1] for i in range(0, len(parts), 2)]
    return parts[0]


def merge_kernel(count, got, out):
    s = sum_of(got).astype(BF16)
    for i in range(count):
        out[i] = s


def total_kernel(got, out):
    out[...] = sum_of(got)


def make_maps(restrict, level, inverse, top, rest):
    r = restrict[...].astype(F32) * 2.0**-5
    for c in range(2):
        one = level[c]
        two = exact(one, one)
        four = exact(two, two)
        eight = exact(four, four)
        head = exact(r, two)
        tail = exact(eight, inverse[c * ROWS : (c + 1) * ROWS, :])
        top[c], rest[c] = halves(exact(head, tail))


def aside_kernel(restrict, level, inverse, outer, middle, inner, top, rest, rel, sems):
    @pl.when(lax.axis_index("z") < EARLY)
    def _():
        make_maps(restrict, level, inverse, top, rest)
        place_tiles(outer, middle, inner, rel, sems)


def late_kernel(restrict, level, inverse, outer, middle, inner, top_in, rest_in, rel_in, top, rest, rel, sems):
    @pl.when(lax.axis_index("z") < EARLY)
    def _():
        top[...] = top_in[...]
        rest[...] = rest_in[...]

    @pl.when(lax.axis_index("z") >= EARLY)
    def _():
        make_maps(restrict, level, inverse, top, rest)
        place_tiles(outer, middle, inner, rel, sems)


def mapped(x, top, rest):
    x_top, x_rest = halves(x)
    return times(x_top, top) + (times(x_top, rest) + times(x_rest, top))


def own_kernel(mine, top, rest, out):
    c = core_index()
    out[...] = mapped(mine[...], top[c], rest[c])


def solve_kernel(part, other, top, rest, out):
    c = 1 - core_index()
    out[...] = part[...] + mapped(other[...], top[c], rest[c])


def shards(right_side, diag_blocks, link_blocks, restrict_map, level_map, coarse_inverse):
    rhs, diag, link = right_side[0], diag_blocks[0], link_blocks[0]
    tile, pack = (VECS, ROWS), (8, ROWS, ROWS)
    to_chip = call(
        pack_kernel,
        bf16(pack),
        [HBM] * 3,
        VMEM,
        (rhs.reshape(8, ROWS, ROWS), diag, link),
        scratch=[pltpu.SemaphoreType.DMA((3,))],
        mib=53.5,
        cost=(0, 1 << 19),
    )
    across = [(1, 2), (2, 1), (3, 4), (4, 3), (5, 6), (6, 5)]
    swap = [(0, 1), (1, 0)]
    to_chip, later = lax.optimization_barrier((to_chip, rhs))
    chip = lax.ppermute(to_chip, ("x", "core"), across)

    rel, state, near, sums, pass_on = call(
        inner_kernel,
        (
            f32((TILES,) + tile),
            f32((3, 8) + tile),
            bf16((8,) + tile),
            f32((2,) + tile),
            bf16((15, ROWS, ROWS)),
        ),
        [VMEM] * 3,
        (VMEM,) * 5,
        (later, diag, link),
        scratch=[
            pltpu.VMEM((TILES,) + tile, F32),
            pltpu.VMEM((TILES,) + tile, F32),
            pltpu.VMEM((2, TILES) + tile, BF16),
            pltpu.VMEM((TILES, 3 * ROWS, ROWS), BF16),
        ],
        mib=24,
        cost=(4 * 10**8, 3 << 20),
    )
    core = lax.ppermute(pass_on, "core", swap)
    outer, part = call(
        outer_kernel,
        (f32((4,) + tile), f32(tile)),
        [VMEM] * 8,
        (VMEM,) * 2,
        (chip, diag, link, state, near, restrict_map, level_map, coarse_inverse),
        scratch=[pltpu.VMEM((8, 3 * ROWS, ROWS), BF16), pltpu.VMEM((4,) + tile, BF16)],
        mib=16,
        cost=(5 * 10**9, 1 << 20),
    )
    middle, copies = call(
        middle_kernel,
        (f32((4,) + tile), bf16((32,) + tile)),
        [VMEM] * 7,
        (VMEM,) * 2,
        (core, diag, link, state, near, sums, part),
        scratch=[
            pltpu.VMEM((8, 3 * ROWS, ROWS), BF16),
            pltpu.VMEM((3, 8) + tile, F32),
            pltpu.VMEM((2, 4) + tile, BF16),
        ],
        mib=16,
        cost=(10**8, 1 << 20),
    )
    copies = lax.all_to_all(copies, ("y", "x"), 0, 0, axis_index_groups=[PLANE], tiled=True)
    copies = call(functools.partial(merge_kernel, 16), bf16((16,) + tile), [VMEM], VMEM, (copies,), cost=(0, 1 << 18))
    wide, whole = bf16((2, ROWS, 2 * ROWS)), f32((TILES,) + tile)
    sources = (restrict_map, level_map, coarse_inverse, outer, middle, rel)
    copies, middle_later = lax.optimization_barrier((copies, middle))
    sources = (restrict_map, level_map, coarse_inverse, outer, middle_later, rel)
    top, rest, out = call(
        aside_kernel,
        (wide, wide, whole),
        [VMEM] * 6,
        (VMEM, VMEM, HBM),
        sources,
        scratch=[pltpu.SemaphoreType.DMA((3,))],
        cost=(10**8, 1 << 20),
    )
    copies, top, rest, out = lax.optimization_barrier((copies, top, rest, out))
    copies = lax.all_to_all(copies, "z", 0, 0, axis_index_groups=[COLUMN], tiled=True)
    copies, late = lax.optimization_barrier((copies, sources))
    top, rest, rel = call(
        late_kernel,
        (wide, wide, whole),
        [VMEM] * 8 + [HBM],
        (VMEM, VMEM, HBM),
        late + (top, rest, out),
        scratch=[pltpu.SemaphoreType.DMA((3,))],
        cost=(10**8, 1 << 20),
        input_output_aliases={8: 2},
    )
    mine = call(total_kernel, f32(tile), [VMEM], VMEM, (copies,), cost=(0, 1 << 17))
    mine, top, rest, rel = lax.optimization_barrier((mine, top, rest, rel))
    other = lax.ppermute(mine, "core", swap)
    solution_shape = f32((VECS, 2 * ROWS))
    part = call(own_kernel, solution_shape, [VMEM] * 3, VMEM, (mine, top, rest), cost=(10**7, 1 << 17))
    solved = call(
        solve_kernel, solution_shape, [VMEM] * 4, VMEM, (part, other, top, rest), cost=(10**7, 1 << 17)
    )
    return (rel[None], solved[None, None])


def solution(mesh):
    fine = Mesh(mesh.devices.reshape(8, 16, 4, 2), ("y", "z", "x", "core"))
    big = P(("y", "z"), ("x", "core"), None, None)
    return jax.shard_map(
        shards,
        mesh=fine,
        in_specs=(big, big, big, P(), P(), P()),
        out_specs=(big, big),
        check_vma=False,
    )
```

```python
import functools

import jax
import jax.numpy as jnp
from jax import lax
from jax.experimental import pallas as pl
from jax.experimental.pallas import tpu as pltpu
from jax.sharding import Mesh
from jax.sharding import PartitionSpec as P

TILES = 32
VECS = 32
ROWS = 128
STEPS = 4
EARLY = 8
HALF = TILES // 2
BF16, F32 = jnp.bfloat16, jnp.float32


def coefficients():
    theta, delta = 2.0, 1.7
    sigma = theta / delta
    rho = 1.0 / sigma
    out = []
    for _ in range(STEPS - 1):
        rho_new = 1.0 / (2.0 * sigma - rho)
        out.append((rho_new * rho, 2.0 * rho_new / delta))
        rho = rho_new
    return out


COEFS = coefficients()
PLANE = [18] + [4 * y + x for y in (0, 1, 7, 2, 6, 3, 5, 4) for x in range(4) if (y, x) != (4, 2)]
COLUMN = [12, 0, 1, 2, 3, 4, 5, 6, 7, 15, 14, 13, 11, 10, 9, 8]
VMEM = pl.BlockSpec(memory_space=pltpu.VMEM)
HBM = pl.BlockSpec(memory_space=pltpu.HBM)
f32 = functools.partial(jax.ShapeDtypeStruct, dtype=F32)
bf16 = functools.partial(jax.ShapeDtypeStruct, dtype=BF16)


def call(kernel, out_shape, in_specs, out_specs, args, scratch=(), mib=8, cost=(0, 0), **kw):
    return pl.pallas_call(
        kernel,
        out_shape=out_shape,
        in_specs=in_specs,
        out_specs=out_specs,
        scratch_shapes=list(scratch),
        compiler_params=pltpu.CompilerParams(vmem_limit_bytes=int(mib * 2**20)),
        cost_estimate=pl.CostEstimate(flops=cost[0], bytes_accessed=cost[1], transcendentals=0),
        **kw,
    )(*args)


def core_index():
    return lax.axis_index("core")


def times(a, b):
    return jnp.dot(a, b, preferred_element_type=F32)


def exact(a, b):
    return jnp.dot(a, b, precision=lax.Precision.HIGHEST, preferred_element_type=F32)


def pack_kernel(rhs, diag, link, out, sems):
    c = core_index()
    parts = (
        (rhs.at[pl.ds(7 * c, 1)], out.at[0:1]),
        (diag.at[pl.ds(29 * c, 3)], out.at[1:4]),
        (link.at[pl.ds(28 * c, 4)], out.at[4:8]),
    )
    copies = [pltpu.make_async_copy(src, dst, sems.at[i]) for i, (src, dst) in enumerate(parts)]
    for copy in copies:
        copy.start()
    for copy in copies:
        copy.wait()


def halves(a):
    top = a.astype(BF16)
    return top, (a - top.astype(F32)).astype(BF16)


def rows(i):
    return slice(i * VECS, (i + 1) * VECS)


def inner_kernel(rhs, diag, link, rel, state, near, sums, pass_on, resid, direc, dirb, stack):
    for t in range(1, TILES - 1):
        stack[t, 0:ROWS] = link[t - 1]
        stack[t, ROWS : 2 * ROWS] = diag[t]
        stack[t, 2 * ROWS :] = link[t].T
    for t in (0, TILES - 1):
        r = rhs[t].astype(F32)
        resid[t] = r
        direc[t] = r * 0.5
        rel[t] = r * 0.5
    totals = [jnp.zeros((VECS, ROWS), F32) for _ in range(2)]
    for k in range(1, STEPS + 1):
        now, later = (k - 1) % 2, k % 2

        def moved(t):
            return rhs[t] if k == 1 else dirb[now, t]

        near[k - 1] = moved(k) * BF16(0.5) if k == 1 else moved(k)
        near[STEPS + k - 1] = moved(TILES - 1 - k) * BF16(0.5) if k == 1 else moved(TILES - 1 - k)
        for t in range(k, TILES - k):
            v = jnp.concatenate([moved(t - 1), moved(t), moved(t + 1)], axis=1)
            a = times(v, stack[t])
            if k == 1:
                before = rhs[t].astype(F32)
                r = before - 0.5 * a
                d = before * 0.5
                total = d
            else:
                r = resid[t] - a
                d = direc[t] if k < STEPS else None
                total = rel[t] if k < STEPS else None
            if k < STEPS:
                c0, c1 = COEFS[k - 1]
                d = c0 * d + c1 * r
                rel[t] = total + d
                dirb[later, t] = d.astype(BF16)
                resid[t] = r
                if k < STEPS - 1 or t == k or t == TILES - 1 - k:
                    direc[t] = d
            else:
                totals[t // HALF] += r.astype(BF16).astype(F32)
    for i, t in enumerate((0, 1, 2, 3, 31, 30, 29, 28)):
        state[0, i] = resid[t]
        state[1, i] = direc[t]
        state[2, i] = rel[t]
    for c in range(2):
        sums[c] = totals[c]

    def fill(diag0, link0, near0, order, group):
        for i in range(4):
            pass_on[i] = diag[diag0 + i]
        for i in range(5):
            pass_on[4 + i] = link[link0 + i]
        for i in range(4):
            pass_on[9, rows(i), :] = near[near0 + i]
            for which in range(2):
                top, rest = halves(state[which, order[i]])
                pass_on[10 + 2 * which, rows(i), :] = top
                pass_on[11 + 2 * which, rows(i), :] = rest
        top, rest = halves(totals[group])
        for i in range(2):
            pass_on[14, rows(2 * i), :] = top
            pass_on[14, rows(2 * i + 1), :] = rest

    @pl.when(core_index() == 0)
    def _():
        fill(28, 27, 4, (7, 6, 5, 4), 1)

    @pl.when(core_index() != 0)
    def _():
        fill(0, 0, 0, (0, 1, 2, 3), 0)


def sweep(k, span, stack, res, dirs, rel, bf):
    for p in span:
        v = jnp.concatenate([bf[p - 1], bf[p], bf[p + 1]], axis=1)
        r = res[p] - times(v, stack[p])
        res[p] = r
        if k < STEPS:
            c0, c1 = COEFS[k - 1]
            dirs[p] = c0 * dirs[p] + c1 * r
            if p in rel:
                rel[p] = rel[p] + dirs[p]


def total(res, span):
    parts = [res[p].astype(BF16).astype(F32) for p in span]
    return (parts[0] + parts[1]) + (parts[2] + parts[3])


ONE, TWO, THREE = slice(0, ROWS), slice(ROWS, 2 * ROWS), slice(2 * ROWS, 3 * ROWS)


def outer_kernel(chip, diag, link, state, near, restrict, level, inverse, edge, part, stack, rhs):
    @pl.when(core_index() == 0)
    def _():
        for i in range(4):
            rhs[i] = chip[0, rows(i), :]
        for p in (1, 2, 3):
            stack[p, ONE] = chip[3 + p]
            stack[p, TWO] = chip[p]
            stack[p, THREE] = chip[4 + p].T
        for i in range(4):
            stack[4 + i, ONE] = chip[7] if i == 0 else link[i - 1]
            stack[4 + i, TWO] = diag[i]
            stack[4 + i, THREE] = link[i].T

    @pl.when(core_index() != 0)
    def _():
        last = link[TILES - 1]
        last = jnp.where(lax.axis_index("x") * 2 + core_index() < 7, last, jnp.zeros_like(last))
        for i in range(4):
            rhs[i] = chip[0, rows(3 - i), :]
        for p in (1, 2, 3):
            stack[p, ONE] = chip[7 - p].T
            stack[p, TWO] = chip[4 - p]
            stack[p, THREE] = last if p == 3 else chip[6 - p]
        for i in range(4):
            stack[4 + i, ONE] = link[31 - i].T
            stack[4 + i, TWO] = diag[31 - i]
            stack[4 + i, THREE] = link[30 - i]

    c = core_index()
    res, dirs, rel = {}, {}, {}
    for p in range(8):
        if p < 4:
            res[p] = rhs[p].astype(F32)
            dirs[p] = res[p] * 0.5
        else:
            res[p] = state[0, 4 * c + (p - 4)]
            dirs[p] = state[1, 4 * c + (p - 4)]
            rel[p] = state[2, 4 * c + (p - 4)]
    for k in range(1, STEPS + 1):
        bf = {p: dirs[p].astype(BF16) for p in range(k - 1, k + 4)}
        bf[k + 4] = near[4 * c + (k - 1)]
        sweep(k, range(k, k + 4), stack, res, dirs, rel, bf)
    part[...] = total(res, range(4, 8))

    @pl.when(c == 0)
    def _():
        for i in range(4):
            edge[i] = rel[4 + i]

    @pl.when(c != 0)
    def _():
        for i in range(4):
            edge[3 - i] = rel[4 + i]


def middle_kernel(core, diag, link, state, near, sums_in, part, edge, copies, stack, mid, ends):
    def received(block, i):
        return core[block, rows(i), :].astype(F32) + core[block + 1, rows(i), :].astype(F32)

    @pl.when(core_index() == 0)
    def _():
        for i in range(4):
            stack[i, ONE] = link[27 + i]
            stack[i, TWO] = diag[28 + i]
            stack[i, THREE] = link[28 + i].T
            stack[4 + i, ONE] = link[31] if i == 0 else core[3 + i]
            stack[4 + i, TWO] = core[i]
            stack[4 + i, THREE] = core[4 + i].T
            for which in range(2):
                mid[which, i] = state[which, 7 - i]
                mid[which, 4 + i] = received(10 + 2 * which, i)
            mid[2, i] = state[2, 7 - i]
            mid[2, 4 + i] = jnp.zeros((VECS, ROWS), F32)
            ends[0, i] = near[4 + i]
            ends[1, i] = core[9, rows(i), :]

    @pl.when(core_index() != 0)
    def _():
        for i in range(4):
            stack[i, ONE] = core[4 + i]
            stack[i, TWO] = core[i]
            stack[i, THREE] = core[5 + i].T
            stack[4 + i, ONE] = core[8] if i == 0 else link[i - 1]
            stack[4 + i, TWO] = diag[i]
            stack[4 + i, THREE] = link[i].T
            for which in range(2):
                mid[which, i] = received(10 + 2 * which, i)
                mid[which, 4 + i] = state[which, i]
            mid[2, i] = jnp.zeros((VECS, ROWS), F32)
            mid[2, 4 + i] = state[2, i]
            ends[0, i] = core[9, rows(i), :]
            ends[1, i] = near[i]

    c = core_index()
    res, dirs, rel = ({p: mid[which, p] for p in range(8)} for which in range(3))
    for k in range(1, STEPS + 1):
        span = range(4 - k, 4 + k)
        bf = {p: dirs[p].astype(BF16) for p in span}
        bf[3 - k] = ends[0, k - 1]
        bf[4 + k] = ends[1, k - 1]
        sweep(k, span, stack, res, dirs, rel, bf)
    beside = jnp.where(c == 0, total(res, range(4, 8)), total(res, range(4)))
    other = core[14, rows(0), :].astype(F32) + core[14, rows(1), :].astype(F32)
    whole = ((sums_in[c] + other) + (part[...] + beside)).astype(BF16)
    for i, place in enumerate(PLANE):
        copies[i] = whole[: VECS // 2] if place % 2 == 0 else whole[VECS // 2 :]

    @pl.when(c == 0)
    def _():
        for i in range(4):
            edge[i] = rel[i]

    @pl.when(c != 0)
    def _():
        for i in range(4):
            edge[i] = rel[4 + i]


def place_tiles(outer, middle, inner, rel, sems):
    c = core_index()
    parts = (
        (outer, rel.at[pl.ds(28 * c, 4)]),
        (inner.at[4:28], rel.at[4:28]),
        (middle, rel.at[pl.ds(28 - 28 * c, 4)]),
    )
    copies = [pltpu.make_async_copy(a, b, sems.at[i]) for i, (a, b) in enumerate(parts)]
    for copy in copies:
        copy.start()
    for copy in copies:
        copy.wait()


def sum_of(ref):
    parts = [ref[i].astype(F32) for i in range(ref.shape[0])]
    while len(parts) > 1:
        parts = [parts[i] + parts[i + 1] for i in range(0, len(parts), 2)]
    return parts[0]


def merge_kernel(count, got, out):
    s = sum_of(got).astype(BF16)
    for i in range(count):
        out[i] = s


def total_kernel(got, out):
    whole = sum_of(got)
    for i in range(out.shape[0]):
        out[i] = whole


def make_maps(restrict, level, inverse, top, rest):
    r = restrict[...].astype(F32) * 2.0**-5
    for c in range(2):
        one = level[c]
        two = exact(one, one)
        four = exact(two, two)
        eight = exact(four, four)
        head = exact(r, two)
        tail = exact(eight, inverse[c * ROWS : (c + 1) * ROWS, :])
        top[c], rest[c] = halves(exact(head, tail))


def aside_kernel(restrict, level, inverse, outer, middle, inner, top, rest, rel, sems):
    @pl.when(lax.axis_index("z") < EARLY)
    def _():
        make_maps(restrict, level, inverse, top, rest)
        place_tiles(outer, middle, inner, rel, sems)


def late_kernel(restrict, level, inverse, outer, middle, inner, top_in, rest_in, rel_in, top, rest, rel, sems):
    @pl.when(lax.axis_index("z") < EARLY)
    def _():
        top[...] = top_in[...]
        rest[...] = rest_in[...]

    @pl.when(lax.axis_index("z") >= EARLY)
    def _():
        make_maps(restrict, level, inverse, top, rest)
        place_tiles(outer, middle, inner, rel, sems)


def mapped(x, top, rest):
    x_top, x_rest = halves(x)
    return times(x_top, top) + (times(x_top, rest) + times(x_rest, top))


def solve_kernel(got, top, rest, out):
    tiles = [jnp.concatenate([got[c], got[2 + c]], axis=0) for c in range(2)]
    out[...] = mapped(tiles[0], top[0], rest[0]) + mapped(tiles[1], top[1], rest[1])


def shards(right_side, diag_blocks, link_blocks, restrict_map, level_map, coarse_inverse):
    rhs, diag, link = right_side[0], diag_blocks[0], link_blocks[0]
    tile, part_tile, pack = (VECS, ROWS), (VECS // 2, ROWS), (8, ROWS, ROWS)
    to_chip = call(
        pack_kernel,
        bf16(pack),
        [HBM] * 3,
        VMEM,
        (rhs.reshape(8, ROWS, ROWS), diag, link),
        scratch=[pltpu.SemaphoreType.DMA((3,))],
        mib=53.5,
        cost=(0, 1 << 19),
    )
    across = [(1, 2), (2, 1), (3, 4), (4, 3), (5, 6), (6, 5)]
    swap = [(0, 1), (1, 0)]
    to_chip, later = lax.optimization_barrier((to_chip, rhs))
    chip = lax.ppermute(to_chip, ("x", "core"), across)

    rel, state, near, sums, pass_on = call(
        inner_kernel,
        (
            f32((TILES,) + tile),
            f32((3, 8) + tile),
            bf16((8,) + tile),
            f32((2,) + tile),
            bf16((15, ROWS, ROWS)),
        ),
        [VMEM] * 3,
        (VMEM,) * 5,
        (later, diag, link),
        scratch=[
            pltpu.VMEM((TILES,) + tile, F32),
            pltpu.VMEM((TILES,) + tile, F32),
            pltpu.VMEM((2, TILES) + tile, BF16),
            pltpu.VMEM((TILES, 3 * ROWS, ROWS), BF16),
        ],
        mib=24,
        cost=(4 * 10**8, 3 << 20),
    )
    core = lax.ppermute(pass_on, "core", swap)
    outer, part = call(
        outer_kernel,
        (f32((4,) + tile), f32(tile)),
        [VMEM] * 8,
        (VMEM,) * 2,
        (chip, diag, link, state, near, restrict_map, level_map, coarse_inverse),
        scratch=[pltpu.VMEM((8, 3 * ROWS, ROWS), BF16), pltpu.VMEM((4,) + tile, BF16)],
        mib=16,
        cost=(5 * 10**9, 1 << 20),
    )
    middle, copies = call(
        middle_kernel,
        (f32((4,) + tile), bf16((32,) + part_tile)),
        [VMEM] * 7,
        (VMEM,) * 2,
        (core, diag, link, state, near, sums, part),
        scratch=[
            pltpu.VMEM((8, 3 * ROWS, ROWS), BF16),
            pltpu.VMEM((3, 8) + tile, F32),
            pltpu.VMEM((2, 4) + tile, BF16),
        ],
        mib=16,
        cost=(10**8, 1 << 20),
    )
    copies = lax.all_to_all(copies, ("y", "x"), 0, 0, axis_index_groups=[PLANE], tiled=True)
    copies = call(functools.partial(merge_kernel, 16), bf16((16,) + part_tile), [VMEM], VMEM, (copies,), cost=(0, 1 << 18))
    wide, whole = bf16((2, ROWS, 2 * ROWS)), f32((TILES,) + tile)
    sources = (restrict_map, level_map, coarse_inverse, outer, middle, rel)
    copies, middle_later = lax.optimization_barrier((copies, middle))
    sources = (restrict_map, level_map, coarse_inverse, outer, middle_later, rel)
    top, rest, out = call(
        aside_kernel,
        (wide, wide, whole),
        [VMEM] * 6,
        (VMEM, VMEM, HBM),
        sources,
        scratch=[pltpu.SemaphoreType.DMA((3,))],
        cost=(10**8, 1 << 20),
    )
    copies, top, rest, out = lax.optimization_barrier((copies, top, rest, out))
    copies = lax.all_to_all(copies, "z", 0, 0, axis_index_groups=[COLUMN], tiled=True)
    copies, late = lax.optimization_barrier((copies, sources))
    top, rest, rel = call(
        late_kernel,
        (wide, wide, whole),
        [VMEM] * 8 + [HBM],
        (VMEM, VMEM, HBM),
        late + (top, rest, out),
        scratch=[pltpu.SemaphoreType.DMA((3,))],
        cost=(10**8, 1 << 20),
        input_output_aliases={8: 2},
    )
    mine = call(total_kernel, f32((4,) + part_tile), [VMEM], VMEM, (copies,), cost=(0, 1 << 17))
    mine, top, rest, rel = lax.optimization_barrier((mine, top, rest, rel))
    mine = lax.all_to_all(mine, ("x", "core"), 0, 0, axis_index_groups=[[0, 1, 2, 3], [4, 5, 6, 7]], tiled=True)
    solved = call(
        solve_kernel, f32((VECS, 2 * ROWS)), [VMEM] * 3, VMEM, (mine, top, rest), cost=(10**7, 1 << 17)
    )
    return (rel[None], solved[None, None])


def solution(mesh):
    fine = Mesh(mesh.devices.reshape(8, 16, 4, 2), ("y", "z", "x", "core"))
    big = P(("y", "z"), ("x", "core"), None, None)
    return jax.shard_map(
        shards,
        mesh=fine,
        in_specs=(big, big, big, P(), P(), P()),
        out_specs=(big, big),
        check_vma=False,
    )
```

```python
import functools

import jax
import jax.numpy as jnp
from jax import lax
from jax.experimental import pallas as pl
from jax.experimental.pallas import tpu as pltpu
from jax.sharding import Mesh
from jax.sharding import PartitionSpec as P

TILES = 32
VECS = 32
ROWS = 128
STEPS = 4
EARLY = 8
HALF = TILES // 2
BF16, F32 = jnp.bfloat16, jnp.float32


def coefficients():
    theta, delta = 2.0, 1.7
    sigma = theta / delta
    rho = 1.0 / sigma
    out = []
    for _ in range(STEPS - 1):
        rho_new = 1.0 / (2.0 * sigma - rho)
        out.append((rho_new * rho, 2.0 * rho_new / delta))
        rho = rho_new
    return out


COEFS = coefficients()
PLANE = [18] + [4 * y + x for y in (0, 1, 7, 2, 6, 3, 5, 4) for x in range(4) if (y, x) != (4, 2)]
COLUMN = [12, 0, 1, 2, 3, 4, 5, 6, 7, 15, 14, 13, 11, 10, 9, 8]
VMEM = pl.BlockSpec(memory_space=pltpu.VMEM)
HBM = pl.BlockSpec(memory_space=pltpu.HBM)
f32 = functools.partial(jax.ShapeDtypeStruct, dtype=F32)
bf16 = functools.partial(jax.ShapeDtypeStruct, dtype=BF16)


def call(kernel, out_shape, in_specs, out_specs, args, scratch=(), mib=8, cost=(0, 0), **kw):
    return pl.pallas_call(
        kernel,
        out_shape=out_shape,
        in_specs=in_specs,
        out_specs=out_specs,
        scratch_shapes=list(scratch),
        compiler_params=pltpu.CompilerParams(vmem_limit_bytes=int(mib * 2**20)),
        cost_estimate=pl.CostEstimate(flops=cost[0], bytes_accessed=cost[1], transcendentals=0),
        **kw,
    )(*args)


def core_index():
    return lax.axis_index("core")


def times(a, b):
    return jnp.dot(a, b, preferred_element_type=F32)


def exact(a, b):
    return jnp.dot(a, b, precision=lax.Precision.HIGHEST, preferred_element_type=F32)


def pack_kernel(rhs, diag, link, out, sems):
    c = core_index()
    parts = (
        (rhs.at[pl.ds(7 * c, 1)], out.at[0:1]),
        (diag.at[pl.ds(29 * c, 3)], out.at[1:4]),
        (link.at[pl.ds(28 * c, 4)], out.at[4:8]),
    )
    copies = [pltpu.make_async_copy(src, dst, sems.at[i]) for i, (src, dst) in enumerate(parts)]
    for copy in copies:
        copy.start()
    for copy in copies:
        copy.wait()


def halves(a):
    top = a.astype(BF16)
    return top, (a - top.astype(F32)).astype(BF16)


def rows(i):
    return slice(i * VECS, (i + 1) * VECS)


def inner_kernel(rhs, diag, link, rel, state, near, sums, pass_on, resid, direc, dirb, stack):
    for t in range(1, TILES - 1):
        stack[t, 0:ROWS] = link[t - 1]
        stack[t, ROWS : 2 * ROWS] = diag[t]
        stack[t, 2 * ROWS :] = link[t].T
    for t in (0, TILES - 1):
        r = rhs[t].astype(F32)
        resid[t] = r
        direc[t] = r * 0.5
        rel[t] = r * 0.5
    totals = [jnp.zeros((VECS, ROWS), F32) for _ in range(2)]
    for k in range(1, STEPS + 1):
        now, later = (k - 1) % 2, k % 2

        def moved(t):
            return rhs[t] if k == 1 else dirb[now, t]

        near[k - 1] = moved(k) * BF16(0.5) if k == 1 else moved(k)
        near[STEPS + k - 1] = moved(TILES - 1 - k) * BF16(0.5) if k == 1 else moved(TILES - 1 - k)
        for t in range(k, TILES - k):
            v = jnp.concatenate([moved(t - 1), moved(t), moved(t + 1)], axis=1)
            a = times(v, stack[t])
            if k == 1:
                before = rhs[t].astype(F32)
                r = before - 0.5 * a
                d = before * 0.5
                total = d
            else:
                r = resid[t] - a
                d = direc[t] if k < STEPS else None
                total = rel[t] if k < STEPS else None
            if k < STEPS:
                c0, c1 = COEFS[k - 1]
                d = c0 * d + c1 * r
                rel[t] = total + d
                dirb[later, t] = d.astype(BF16)
                resid[t] = r
                if k < STEPS - 1 or t == k or t == TILES - 1 - k:
                    direc[t] = d
            else:
                totals[t // HALF] += r.astype(BF16).astype(F32)
    for i, t in enumerate((0, 1, 2, 3, 31, 30, 29, 28)):
        state[0, i] = resid[t]
        state[1, i] = direc[t]
        state[2, i] = rel[t]
    for c in range(2):
        sums[c] = totals[c]

    def fill(diag0, link0, near0, order, group):
        for i in range(4):
            pass_on[i] = diag[diag0 + i]
        for i in range(5):
            pass_on[4 + i] = link[link0 + i]
        for i in range(4):
            pass_on[9, rows(i), :] = near[near0 + i]
            for which in range(2):
                top, rest = halves(state[which, order[i]])
                pass_on[10 + 2 * which, rows(i), :] = top
                pass_on[11 + 2 * which, rows(i), :] = rest
        top, rest = halves(totals[group])
        for i in range(2):
            pass_on[14, rows(2 * i), :] = top
            pass_on[14, rows(2 * i + 1), :] = rest

    @pl.when(core_index() == 0)
    def _():
        fill(28, 27, 4, (7, 6, 5, 4), 1)

    @pl.when(core_index() != 0)
    def _():
        fill(0, 0, 0, (0, 1, 2, 3), 0)


def sweep(k, span, stack, res, dirs, rel, bf):
    for p in span:
        v = jnp.concatenate([bf[p - 1], bf[p], bf[p + 1]], axis=1)
        r = res[p] - times(v, stack[p])
        res[p] = r
        if k < STEPS:
            c0, c1 = COEFS[k - 1]
            dirs[p] = c0 * dirs[p] + c1 * r
            if p in rel:
                rel[p] = rel[p] + dirs[p]


def total(res, span):
    parts = [res[p].astype(BF16).astype(F32) for p in span]
    return (parts[0] + parts[1]) + (parts[2] + parts[3])


ONE, TWO, THREE = slice(0, ROWS), slice(ROWS, 2 * ROWS), slice(2 * ROWS, 3 * ROWS)


def outer_kernel(chip, diag, link, state, near, restrict, level, inverse, edge, part, stack, rhs):
    @pl.when(core_index() == 0)
    def _():
        for i in range(4):
            rhs[i] = chip[0, rows(i), :]
        for p in (1, 2, 3):
            stack[p, ONE] = chip[3 + p]
            stack[p, TWO] = chip[p]
            stack[p, THREE] = chip[4 + p].T
        for i in range(4):
            stack[4 + i, ONE] = chip[7] if i == 0 else link[i - 1]
            stack[4 + i, TWO] = diag[i]
            stack[4 + i, THREE] = link[i].T

    @pl.when(core_index() != 0)
    def _():
        last = link[TILES - 1]
        last = jnp.where(lax.axis_index("x") * 2 + core_index() < 7, last, jnp.zeros_like(last))
        for i in range(4):
            rhs[i] = chip[0, rows(3 - i), :]
        for p in (1, 2, 3):
            stack[p, ONE] = chip[7 - p].T
            stack[p, TWO] = chip[4 - p]
            stack[p, THREE] = last if p == 3 else chip[6 - p]
        for i in range(4):
            stack[4 + i, ONE] = link[31 - i].T
            stack[4 + i, TWO] = diag[31 - i]
            stack[4 + i, THREE] = link[30 - i]

    c = core_index()
    res, dirs, rel = {}, {}, {}
    for p in range(8):
        if p < 4:
            res[p] = rhs[p].astype(F32)
            dirs[p] = res[p] * 0.5
        else:
            res[p] = state[0, 4 * c + (p - 4)]
            dirs[p] = state[1, 4 * c + (p - 4)]
            rel[p] = state[2, 4 * c + (p - 4)]
    for k in range(1, STEPS + 1):
        bf = {p: dirs[p].astype(BF16) for p in range(k - 1, k + 4)}
        bf[k + 4] = near[4 * c + (k - 1)]
        sweep(k, range(k, k + 4), stack, res, dirs, rel, bf)
    part[...] = total(res, range(4, 8))

    @pl.when(c == 0)
    def _():
        for i in range(4):
            edge[i] = rel[4 + i]

    @pl.when(c != 0)
    def _():
        for i in range(4):
            edge[3 - i] = rel[4 + i]


def middle_kernel(core, diag, link, state, near, sums_in, part, edge, copies, stack, mid, ends):
    def received(block, i):
        return core[block, rows(i), :].astype(F32) + core[block + 1, rows(i), :].astype(F32)

    @pl.when(core_index() == 0)
    def _():
        for i in range(4):
            stack[i, ONE] = link[27 + i]
            stack[i, TWO] = diag[28 + i]
            stack[i, THREE] = link[28 + i].T
            stack[4 + i, ONE] = link[31] if i == 0 else core[3 + i]
            stack[4 + i, TWO] = core[i]
            stack[4 + i, THREE] = core[4 + i].T
            for which in range(2):
                mid[which, i] = state[which, 7 - i]
                mid[which, 4 + i] = received(10 + 2 * which, i)
            mid[2, i] = state[2, 7 - i]
            mid[2, 4 + i] = jnp.zeros((VECS, ROWS), F32)
            ends[0, i] = near[4 + i]
            ends[1, i] = core[9, rows(i), :]

    @pl.when(core_index() != 0)
    def _():
        for i in range(4):
            stack[i, ONE] = core[4 + i]
            stack[i, TWO] = core[i]
            stack[i, THREE] = core[5 + i].T
            stack[4 + i, ONE] = core[8] if i == 0 else link[i - 1]
            stack[4 + i, TWO] = diag[i]
            stack[4 + i, THREE] = link[i].T
            for which in range(2):
                mid[which, i] = received(10 + 2 * which, i)
                mid[which, 4 + i] = state[which, i]
            mid[2, i] = jnp.zeros((VECS, ROWS), F32)
            mid[2, 4 + i] = state[2, i]
            ends[0, i] = core[9, rows(i), :]
            ends[1, i] = near[i]

    c = core_index()
    res, dirs, rel = ({p: mid[which, p] for p in range(8)} for which in range(3))
    for k in range(1, STEPS + 1):
        span = range(4 - k, 4 + k)
        bf = {p: dirs[p].astype(BF16) for p in span}
        bf[3 - k] = ends[0, k - 1]
        bf[4 + k] = ends[1, k - 1]
        sweep(k, span, stack, res, dirs, rel, bf)
    beside = jnp.where(c == 0, total(res, range(4, 8)), total(res, range(4)))
    other = core[14, rows(0), :].astype(F32) + core[14, rows(1), :].astype(F32)
    whole = ((sums_in[c] + other) + (part[...] + beside)).astype(BF16)
    for i, place in enumerate(PLANE):
        copies[i] = whole[: VECS // 2] if place % 2 == 0 else whole[VECS // 2 :]

    @pl.when(c == 0)
    def _():
        for i in range(4):
            edge[i] = rel[i]

    @pl.when(c != 0)
    def _():
        for i in range(4):
            edge[i] = rel[4 + i]


def place_tiles(outer, middle, inner, rel, sems):
    c = core_index()
    parts = (
        (outer, rel.at[pl.ds(28 * c, 4)]),
        (inner.at[4:28], rel.at[4:28]),
        (middle, rel.at[pl.ds(28 - 28 * c, 4)]),
    )
    copies = [pltpu.make_async_copy(a, b, sems.at[i]) for i, (a, b) in enumerate(parts)]
    for copy in copies:
        copy.start()
    for copy in copies:
        copy.wait()


def sum_of(ref):
    parts = [ref[i].astype(F32) for i in range(ref.shape[0])]
    while len(parts) > 1:
        parts = [parts[i] + parts[i + 1] for i in range(0, len(parts), 2)]
    return parts[0]


def merge_kernel(count, got, out):
    s = sum_of(got).astype(BF16)
    for i in range(count):
        out[i] = s


def total_kernel(got, out):
    whole = sum_of(got)
    for i in range(out.shape[0]):
        out[i] = whole


def make_maps(restrict, level, inverse, top, rest):
    r = restrict[...].astype(F32) * 2.0**-5
    for c in range(2):
        one = level[c]
        two = exact(one, one)
        four = exact(two, two)
        eight = exact(four, four)
        head = exact(r, two)
        tail = exact(eight, inverse[c * ROWS : (c + 1) * ROWS, :])
        top[c], rest[c] = halves(exact(head, tail))


def aside_kernel(restrict, level, inverse, outer, middle, inner, top, rest, rel, sems):
    @pl.when(lax.axis_index("z") < EARLY)
    def _():
        make_maps(restrict, level, inverse, top, rest)
        place_tiles(outer, middle, inner, rel, sems)


def late_kernel(restrict, level, inverse, outer, middle, inner, top_in, rest_in, rel_in, top, rest, rel, sems):
    @pl.when(lax.axis_index("z") < EARLY)
    def _():
        top[...] = top_in[...]
        rest[...] = rest_in[...]

    @pl.when(lax.axis_index("z") >= EARLY)
    def _():
        make_maps(restrict, level, inverse, top, rest)
        place_tiles(outer, middle, inner, rel, sems)


def mapped(x, top, rest):
    x_top, x_rest = halves(x)
    return times(x_top, top) + (times(x_top, rest) + times(x_rest, top))


def solve_kernel(got, top, rest, out):
    tiles = [jnp.concatenate([got[u], got[d]], axis=0) for u, d in ((1, 0), (2, 3))]
    out[...] = mapped(tiles[0], top[0], rest[0]) + mapped(tiles[1], top[1], rest[1])


def shards(right_side, diag_blocks, link_blocks, restrict_map, level_map, coarse_inverse):
    rhs, diag, link = right_side[0], diag_blocks[0], link_blocks[0]
    tile, part_tile, pack = (VECS, ROWS), (VECS // 2, ROWS), (8, ROWS, ROWS)
    to_chip = call(
        pack_kernel,
        bf16(pack),
        [HBM] * 3,
        VMEM,
        (rhs.reshape(8, ROWS, ROWS), diag, link),
        scratch=[pltpu.SemaphoreType.DMA((3,))],
        mib=53.5,
        cost=(0, 1 << 19),
    )
    across = [(1, 2), (2, 1), (3, 4), (4, 3), (5, 6), (6, 5)]
    swap = [(0, 1), (1, 0)]
    to_chip, later = lax.optimization_barrier((to_chip, rhs))
    chip = lax.ppermute(to_chip, ("x", "core"), across)

    rel, state, near, sums, pass_on = call(
        inner_kernel,
        (
            f32((TILES,) + tile),
            f32((3, 8) + tile),
            bf16((8,) + tile),
            f32((2,) + tile),
            bf16((15, ROWS, ROWS)),
        ),
        [VMEM] * 3,
        (VMEM,) * 5,
        (later, diag, link),
        scratch=[
            pltpu.VMEM((TILES,) + tile, F32),
            pltpu.VMEM((TILES,) + tile, F32),
            pltpu.VMEM((2, TILES) + tile, BF16),
            pltpu.VMEM((TILES, 3 * ROWS, ROWS), BF16),
        ],
        mib=24,
        cost=(4 * 10**8, 3 << 20),
    )
    core = lax.ppermute(pass_on, "core", swap)
    outer, part = call(
        outer_kernel,
        (f32((4,) + tile), f32(tile)),
        [VMEM] * 8,
        (VMEM,) * 2,
        (chip, diag, link, state, near, restrict_map, level_map, coarse_inverse),
        scratch=[pltpu.VMEM((8, 3 * ROWS, ROWS), BF16), pltpu.VMEM((4,) + tile, BF16)],
        mib=16,
        cost=(5 * 10**9, 1 << 20),
    )
    middle, copies = call(
        middle_kernel,
        (f32((4,) + tile), bf16((32,) + part_tile)),
        [VMEM] * 7,
        (VMEM,) * 2,
        (core, diag, link, state, near, sums, part),
        scratch=[
            pltpu.VMEM((8, 3 * ROWS, ROWS), BF16),
            pltpu.VMEM((3, 8) + tile, F32),
            pltpu.VMEM((2, 4) + tile, BF16),
        ],
        mib=16,
        cost=(10**8, 1 << 20),
    )
    copies = lax.all_to_all(copies, ("y", "x"), 0, 0, axis_index_groups=[PLANE], tiled=True)
    copies = call(functools.partial(merge_kernel, 16), bf16((16,) + part_tile), [VMEM], VMEM, (copies,), cost=(0, 1 << 18))
    wide, whole = bf16((2, ROWS, 2 * ROWS)), f32((TILES,) + tile)
    sources = (restrict_map, level_map, coarse_inverse, outer, middle, rel)
    copies, middle_later = lax.optimization_barrier((copies, middle))
    sources = (restrict_map, level_map, coarse_inverse, outer, middle_later, rel)
    top, rest, out = call(
        aside_kernel,
        (wide, wide, whole),
        [VMEM] * 6,
        (VMEM, VMEM, HBM),
        sources,
        scratch=[pltpu.SemaphoreType.DMA((3,))],
        cost=(10**8, 1 << 20),
    )
    copies, top, rest, out = lax.optimization_barrier((copies, top, rest, out))
    copies = lax.all_to_all(copies, "z", 0, 0, axis_index_groups=[COLUMN], tiled=True)
    copies, late = lax.optimization_barrier((copies, sources))
    top, rest, rel = call(
        late_kernel,
        (wide, wide, whole),
        [VMEM] * 8 + [HBM],
        (VMEM, VMEM, HBM),
        late + (top, rest, out),
        scratch=[pltpu.SemaphoreType.DMA((3,))],
        cost=(10**8, 1 << 20),
        input_output_aliases={8: 2},
    )
    mine = call(total_kernel, f32((4,) + part_tile), [VMEM], VMEM, (copies,), cost=(0, 1 << 17))
    mine, top, rest, rel = lax.optimization_barrier((mine, top, rest, rel))
    mine = lax.all_to_all(mine, ("x", "core"), 0, 0, axis_index_groups=[[2, 0, 1, 3], [6, 4, 5, 7]], tiled=True)
    solved = call(
        solve_kernel, f32((VECS, 2 * ROWS)), [VMEM] * 3, VMEM, (mine, top, rest), cost=(10**7, 1 << 17)
    )
    return (rel[None], solved[None, None])


def solution(mesh):
    fine = Mesh(mesh.devices.reshape(8, 16, 4, 2), ("y", "z", "x", "core"))
    big = P(("y", "z"), ("x", "core"), None, None)
    return jax.shard_map(
        shards,
        mesh=fine,
        in_specs=(big, big, big, P(), P(), P()),
        out_specs=(big, big),
        check_vma=False,
    )
```
